32 devices in a mesh: req: 4 (over y, x), blk: 8 (over z, core).
Axes of the slice: x: 2, y: 2, z: 4, core: 2. Of those that a mesh axis runs over, the one named last changes fastest.
Arguments:
- hyper_state: float32 [32, 4, 2048], P(('req', 'blk')), may hold values from -6 to 6
- lengths: int32 [32], P('req'), may hold values from 1 to 16384
- key_cache: bfloat16 [32, 16, 2052, 128], P('req', 'blk'), may hold values from -360 to 360
- value_cache: bfloat16 [32, 16, 2052, 128], P('req', 'blk'), may hold values from -6 to 6
- attn_in_weight: bfloat16 [3, 2048, 2048], P(None, None, 'blk'), may hold values from -0.125 to 0.125
- attn_out_weight: bfloat16 [2048, 2048], P('blk'), may hold values from -0.125 to 0.125
- w_gate: bfloat16 [2048, 8192], P('req', 'blk'), may hold values from -0.125 to 0.125
- w_up: bfloat16 [2048, 8192], P('req', 'blk'), may hold values from -0.125 to 0.125
- w_down: bfloat16 [8192, 2048], P('blk', 'req'), may hold values from -0.0625 to 0.0625
- width_in: float32 [2, 4], replicated, may hold values from 0.2 to 1
- stream_mix: float32 [2, 4, 4], replicated, may hold values from -0.6 to 0.6
- depth_out: float32 [2, 4], replicated, may hold values from 0.5 to 1.5
Outputs:
- hyper_out: float32 [32, 4, 2048], P(('req', 'blk'))
The draws below stay inside these ranges and needn't reach their ends.
All inputs are finite; a program needn't handle non-finite values.
Results may differ from the reference program's by a relative error of at most 0.023.
Values may be sent and summed in bfloat16 or wider, within the bound.
A program may use at most 128 MiB of HBM per device.

```python
import math
import jax
import jax.numpy as jnp
from jax import lax

D = 2048
HEADS = 16
HEAD = 128
FF = 8192
STREAMS = 4
MAXLEN = 16385
REQUESTS = 32
SLOTS = 2052


def draw_key_cache(key, part):
    noise = jax.random.normal(key, (REQUESTS, HEADS, SLOTS, HEAD), jnp.float32)
    noise = jnp.clip(noise, -6.0, 6.0)
    factor = 2.5
    return (noise * factor).astype(jnp.bfloat16)


def place_ends(result, stream_key, least, high):
    dims = result.shape
    spot = [jax.random.randint(jax.random.fold_in(stream_key, axis), (), 0, dims[axis]) for axis in range(len(dims))]
    result = result.at[tuple(spot)].set(least)
    longest = dims.index(max(dims))
    spot[longest] = (spot[longest] + 1) % dims[longest]
    return result.at[tuple(spot)].set(high)


def shard_levels(rng, shape, pieces, least, largest):
    def one(position, shards_of):
        heights = jax.random.uniform(jax.random.fold_in(jax.random.fold_in(rng, 6), position), (shards_of,), jnp.float32, least / len(pieces), largest / len(pieces))
        return jnp.repeat(jnp.exp(heights), shape[position] // shards_of).reshape((-1,) + (1,) * (len(shape) - position - 1))

    loudness = one(*pieces[0])
    for cut in pieces[1:]:
        loudness = loudness * one(*cut)
    return loudness


def bell_draw(key, extent, scale, most, shards=(), dtype=jnp.bfloat16):
    array = jax.random.normal(key, extent, jnp.float32) * scale
    if len(shards) > 0:
        array = shard_levels(key, extent, shards, -0.22, 0.18) * array
    return jnp.clip(array, min=-most, max=most).astype(dtype)


def setup_inputs(seed: int = 0) -> dict:
    key_list = jax.random.split(jax.random.key(seed), 13)
    return {
        "hyper_state": bell_draw(key_list[0], (REQUESTS, STREAMS, D), 1.0, 6.0, ((0, 32),), jnp.float32),
        "lengths": place_ends(jax.random.randint(key_list[1], (REQUESTS,), 1, MAXLEN), jax.random.fold_in(key_list[1], 1), 1, MAXLEN - 1).astype(jnp.int32),
        "key_cache": draw_key_cache(jax.random.fold_in(key_list[12], 71), 0),
        "value_cache": bell_draw(key_list[3], (REQUESTS, HEADS, SLOTS, HEAD), 1.0, 6.0, ((0, 4), (1, 8))),
        "attn_in_weight": bell_draw(key_list[4], (3, D, D), D ** -0.5, 0.125, ((2, 8),)),
        "attn_out_weight": bell_draw(key_list[5], (D, D), D ** -0.5, 0.125, ((0, 8),)),
        "w_gate": bell_draw(key_list[6], (D, FF), D ** -0.5, 0.125, ((0, 4), (1, 8))),
        "w_up": bell_draw(key_list[7], (D, FF), D ** -0.5, 0.125, ((0, 4), (1, 8))),
        "w_down": bell_draw(key_list[8], (FF, D), FF ** -0.5, 0.0625, ((0, 8), (1, 4))),
        "width_in": jnp.clip(jax.random.uniform(key_list[9], (2, STREAMS), jnp.float32, 0.2, 1.0), 0.2, 1.0),
        "stream_mix": jnp.clip(jax.random.uniform(key_list[10], (2, STREAMS, STREAMS), jnp.float32, -0.6, 0.6), -0.6, 0.6),
        "depth_out": jnp.clip(jax.random.uniform(key_list[11], (2, STREAMS), jnp.float32, 0.5, 1.5), 0.5, 1.5),
    }


def layer_norm(values):
    center = values - lax.optimization_barrier(jnp.mean(values, axis=-1, keepdims=True))
    spread = lax.optimization_barrier(jnp.mean(center * center, axis=-1, keepdims=True))
    return center * lax.rsqrt(spread + 1e-05)

def combine(state, weights):
    return lax.optimization_barrier(jnp.sum(state * weights[None, :, None], axis=1))

def remix(state, matrix):
    return lax.optimization_barrier(jnp.sum(state[:, :, None, :] * matrix[None, :, :, None], axis=1))

def rotate(values, positions):
    half = values.shape[-1] // 2
    index = jnp.arange(half).astype(jnp.float32)
    freqs = jnp.exp(index * (-2.0 * math.log(10000.0) / values.shape[-1]))
    angles = positions.astype(jnp.float32)[:, None, None] * freqs[None, None, :]
    cosine = jnp.cos(angles)
    sine = jnp.sin(angles)
    first = values[..., :half]
    second = values[..., half:]
    return jnp.concatenate([first * cosine - second * sine, second * cosine + first * sine], axis=-1)

def attend_one(item):
    query, key_new, value_new, keys, values, length = item
    scale = query.shape[-1] ** (-0.5)
    query_wide = query.astype(jnp.float32)
    scores = jnp.einsum('he,hse->hs', query_wide, keys.astype(jnp.float32)) * scale
    own = lax.optimization_barrier(jnp.sum(query_wide * key_new.astype(jnp.float32), axis=-1)) * scale
    valid = jnp.arange(keys.shape[1]).astype(jnp.int32)[None, :] < length
    peak = jnp.maximum(lax.optimization_barrier(jnp.max(jnp.where(valid, scores, -jnp.inf), axis=-1)), own)
    shares = jnp.where(valid, jnp.exp(scores - peak[:, None]), 0.0)
    own_share = jnp.exp(own - peak)
    denom = lax.optimization_barrier(jnp.sum(shares, axis=-1)) + own_share
    probs = (shares / denom[:, None]).astype(jnp.bfloat16)
    own_prob = (own_share / denom).astype(jnp.bfloat16)
    mixed = jnp.einsum('hs,hse->he', probs.astype(jnp.float32), values.astype(jnp.float32))
    mixed = mixed + own_prob.astype(jnp.float32)[:, None] * value_new.astype(jnp.float32)
    return mixed.astype(jnp.bfloat16)

def reference(hyper_state, lengths, key_cache, value_cache, attn_in_weight, attn_out_weight, w_gate, w_up, w_down, width_in, stream_mix, depth_out):
    state = hyper_state
    normed = layer_norm(combine(state, width_in[0])).astype(jnp.bfloat16)
    count = normed.shape[0]
    projected = [jnp.dot(normed, attn_in_weight[index], preferred_element_type=jnp.float32) for index in range(3)]
    query = rotate(projected[0].reshape(count, HEADS, HEAD), lengths).astype(jnp.bfloat16)
    key_new = rotate(projected[1].reshape(count, HEADS, HEAD), lengths).astype(jnp.bfloat16)
    value_new = projected[2].reshape(count, HEADS, HEAD).astype(jnp.bfloat16)
    attended = lax.map(attend_one, (query, key_new, value_new, key_cache, value_cache, lengths))
    flat = attended.reshape(count, HEADS * HEAD)
    attn_out = jnp.dot(flat, attn_out_weight, preferred_element_type=jnp.float32)
    state = remix(state, stream_mix[0]) + depth_out[0][None, :, None] * attn_out[:, None, :]
    normed_mlp = layer_norm(combine(state, width_in[1])).astype(jnp.bfloat16)
    gate = jnp.dot(normed_mlp, w_gate, preferred_element_type=jnp.float32)
    upward = jnp.dot(normed_mlp, w_up, preferred_element_type=jnp.float32)
    hidden = (jax.nn.silu(gate) * upward).astype(jnp.bfloat16)
    mlp_out = jnp.dot(hidden, w_down, preferred_element_type=jnp.float32)
    return remix(state, stream_mix[1]) + depth_out[1][None, :, None] * mlp_out[:, None, :]
```

```python
import functools
import math

import jax
import jax.numpy as jnp
import numpy as np
from jax import lax
from jax.experimental import pallas as pl
from jax.experimental.pallas import tpu as pltpu
from jax.sharding import PartitionSpec as P

MESH = pl.DeviceIdType.MESH
LANES = 128
F32 = jnp.float32
BF16 = jnp.bfloat16


def split_two_pi():
    whole = 2.0 * math.pi
    one = float(np.round(whole * 2.0**8) / 2.0**8)
    two = float(np.round((whole - one) * 2.0**20) / 2.0**20)
    return one, two, whole - one - two


def sine_cosine(angles):
    one, two, three = split_two_pi()
    turns = jnp.floor(angles * (1.0 / (2.0 * math.pi)) + 0.5)
    rest = ((angles - turns * one) - turns * two) - turns * three
    return jnp.sin(rest), jnp.cos(rest)


def normalize(row):
    count = row.shape[0] * row.shape[1]
    center = row - jnp.sum(row, keepdims=True) * (1.0 / count)
    spread = jnp.sum(center * center, keepdims=True) * (1.0 / count)
    return center * lax.rsqrt(spread + 1e-05)


def gather_lanes(ref):
    return jnp.concatenate([ref[:, k, :] for k in range(ref.shape[1])], axis=1)


def scatter_lanes(ref, values):
    for k in range(ref.shape[1]):
        ref[:, k, :] = values[:, k * LANES : (k + 1) * LANES]


def wait_bytes(ref, sem):
    pltpu.make_async_copy(ref, ref, sem).wait()


def layer_kernel(
    req_count,
    blk_count,
    hyper_ref,
    lengths_ref,
    freq_ref,
    width_ref,
    mix_ref,
    depth_ref,
    keys_hbm,
    values_hbm,
    win_hbm,
    wout_hbm,
    wgate_hbm,
    wup_hbm,
    wdown_hbm,
    out_ref,
    keys,
    values,
    win,
    wout,
    wgate,
    wup,
    wdown,
    streams,
    row_send,
    row_recv,
    attn_send,
    attn_recv,
    norm_send,
    norm_recv,
    gate_send,
    gate_recv,
    hid_send,
    hid_recv,
    down_send,
    down_recv,
    mlp_row,
    load_sem,
    key_sem,
    value_sem,
    blk_send_sem,
    blk_recv_sem,
    req_send_sem,
    req_recv_sem,
    all_send_sem,
    all_recv_sem,
):
    req = lax.axis_index("req")
    blk = lax.axis_index("blk")
    everyone = req_count * blk_count
    me = req * blk_count + blk
    group, heads, slots, head = keys.shape

    loads = [pltpu.make_async_copy(win_hbm.at[k], win.at[k], load_sem.at[k]) for k in range(3)]
    key_loads = [
        pltpu.make_async_copy(keys_hbm.at[r], keys.at[r], key_sem.at[r]) for r in range(group)
    ]
    value_loads = [
        pltpu.make_async_copy(values_hbm.at[r], values.at[r], value_sem.at[r])
        for r in range(group)
    ]
    late = [
        pltpu.make_async_copy(src, dst, load_sem.at[3 + i])
        for i, (src, dst) in enumerate(
            [(wout_hbm, wout), (wgate_hbm, wgate), (wup_hbm, wup), (wdown_hbm, wdown)]
        )
    ]
    barrier = pltpu.get_barrier_semaphore()

    def greet(i, carry):
        other = lax.rem(me + i, everyone)
        pl.semaphore_signal(
            barrier,
            inc=1,
            device_id=(other // blk_count, lax.rem(other, blk_count)),
            device_id_type=MESH,
        )
        return carry

    lax.fori_loop(1, everyone, greet, 0)
    for copy in loads + key_loads + value_loads + late:
        copy.start()

    for k in range(streams.shape[1]):
        streams[:, k, :] = hyper_ref[0, :, k * LANES : (k + 1) * LANES]
    count = streams.shape[0]
    state = [streams[s] for s in range(count)]
    row = functools.reduce(lambda a, b: a + b, [state[s] * width_ref[0, s] for s in range(count)])
    row_send[...] = normalize(row)

    pl.semaphore_wait(barrier, everyone - 1)

    def blk_exchange(phase, source_of, landing):
        copies = []
        for d in range(1, blk_count):
            other = lax.rem(blk + d, blk_count)
            copy = pltpu.make_async_remote_copy(
                src_ref=source_of(other),
                dst_ref=landing.at[blk],
                send_sem=blk_send_sem.at[phase, d - 1],
                recv_sem=blk_recv_sem.at[phase, d - 1],
                device_id=(req, other),
                device_id_type=MESH,
            )
            copy.start()
            copies.append(copy)
        return copies

    def blk_arrivals(phase, source_of, landing):
        for d in range(1, blk_count):
            other = lax.rem(blk + blk_count - d, blk_count)
            pltpu.make_async_remote_copy(
                src_ref=source_of(other),
                dst_ref=landing.at[other],
                send_sem=blk_send_sem.at[phase, d - 1],
                recv_sem=blk_recv_sem.at[phase, d - 1],
                device_id=(req, other),
                device_id_type=MESH,
            ).wait_recv()

    def req_exchange(phase, source_of, landing):
        copies = []
        for d in range(1, req_count):
            other = lax.rem(req + d, req_count)
            copy = pltpu.make_async_remote_copy(
                src_ref=source_of(other),
                dst_ref=landing.at[req],
                send_sem=req_send_sem.at[phase, d - 1],
                recv_sem=req_recv_sem.at[phase, d - 1],
                device_id=(other, blk),
                device_id_type=MESH,
            )
            copy.start()
            copies.append(copy)
        return copies

    def req_arrivals(phase, source_of, landing):
        for d in range(1, req_count):
            other = lax.rem(req + req_count - d, req_count)
            pltpu.make_async_remote_copy(
                src_ref=source_of(other),
                dst_ref=landing.at[other],
                send_sem=req_send_sem.at[phase, d - 1],
                recv_sem=req_recv_sem.at[phase, d - 1],
                device_id=(other, blk),
                device_id_type=MESH,
            ).wait_recv()

    def all_exchange(phase, source_of, landing):
        def send(i, carry):
            other = lax.rem(me + i, everyone)
            other_req = other // blk_count
            pltpu.make_async_remote_copy(
                src_ref=source_of(other, other_req),
                dst_ref=landing.at[me],
                send_sem=all_send_sem.at[phase],
                recv_sem=all_recv_sem.at[phase],
                device_id=(other_req, lax.rem(other, blk_count)),
                device_id_type=MESH,
            ).start()
            return carry

        lax.fori_loop(1, everyone, send, 0)

    def finish(copies):
        for copy in copies:
            copy.wait_send()

    row_copies = blk_exchange(0, lambda other: row_send, row_recv)
    row_recv[blk] = row_send[...]

    row_at = lax.broadcasted_iota(jnp.int32, (group, 1), 0)
    lengths = jnp.zeros((group, 1), jnp.int32)
    for r in range(group):
        lengths = jnp.where(row_at == r, lengths_ref[r], lengths)
    angles = lengths.astype(F32) * freq_ref[...]
    sine, cosine = sine_cosine(angles)
    lane = lax.broadcasted_iota(jnp.int32, (group, head), 1)
    sine = jnp.where(lane < head // 2, -sine, sine)

    def rotate(part):
        return (part * cosine + pltpu.roll(part, head // 2, 1) * sine).astype(BF16)

    mixed_state = [
        functools.reduce(lambda a, b: a + b, [state[s] * mix_ref[0, s, t] for s in range(count)])
        for t in range(count)
    ]

    blk_arrivals(0, lambda other: row_send, row_recv)
    normed = gather_lanes(row_recv).astype(BF16)
    projected = []
    for k in range(3):
        loads[k].wait()
        projected.append(jnp.dot(normed, win[k], preferred_element_type=F32))
    finish(row_copies)

    scale = head ** (-0.5)
    heads_of = [slice(h * head, (h + 1) * head) for h in range(heads)]
    query = [rotate(projected[0][:, part]) for part in heads_of]
    key_new = [rotate(projected[1][:, part]) for part in heads_of]
    value_new = [projected[2][:, part].astype(BF16).astype(F32) for part in heads_of]
    scores = [None] * heads
    for r in range(group):
        key_loads[r].wait()
        for h in range(heads):
            part = lax.dot_general(
                query[h], keys[r, h], (((1,), (1,)), ((), ())), preferred_element_type=F32
            )
            scores[h] = part if r == 0 else jnp.where(row_at == r, part, scores[h])
    slot = lax.broadcasted_iota(jnp.int32, (group, slots), 1)
    shares, own_share, denom = [], [], []
    for h in range(heads):
        own = scale * jnp.sum(
            query[h].astype(F32) * key_new[h].astype(F32), axis=-1, keepdims=True
        )
        masked = jnp.where(slot < lengths, scores[h] * scale, -jnp.inf)
        peak = jnp.maximum(jnp.max(masked, axis=-1, keepdims=True), own)
        share = jnp.exp(masked - peak)
        own_share.append(jnp.exp(own - peak))
        denom.append(jnp.sum(share, axis=-1, keepdims=True) + own_share[h])
        shares.append(share.astype(BF16))
    mixed = [None] * heads
    for r in range(group):
        value_loads[r].wait()
        for h in range(heads):
            part = jnp.dot(shares[h], values[r, h], preferred_element_type=F32)
            mixed[h] = part if r == 0 else jnp.where(row_at == r, part, mixed[h])
    flat = jnp.concatenate(
        [(mixed[h] + own_share[h] * value_new[h]) / denom[h] for h in range(heads)], axis=1
    ).astype(BF16)
    late[0].wait()
    scatter_lanes(attn_send, jnp.dot(flat, wout[...], preferred_element_type=F32))

    attn_copies = blk_exchange(1, lambda other: attn_send.at[other], attn_recv)
    attn_recv[blk] = attn_send[blk]
    blk_arrivals(1, lambda other: attn_send.at[other], attn_recv)
    attn_out = functools.reduce(lambda a, b: a + b, [attn_recv[j] for j in range(blk_count)])
    state = [mixed_state[t] + depth_ref[0, t] * attn_out for t in range(count)]
    row = functools.reduce(lambda a, b: a + b, [state[s] * width_ref[1, s] for s in range(count)])
    row = normalize(row)
    chunk = norm_send.shape[1]
    for c in range(req_count):
        norm_send[c] = row[c * chunk : (c + 1) * chunk]

    all_exchange(0, lambda other, other_req: norm_send.at[other_req], norm_recv)
    norm_recv[me] = norm_send[req]
    finish(attn_copies)
    mixed_state = [
        functools.reduce(lambda a, b: a + b, [state[s] * mix_ref[1, s, t] for s in range(count)])
        for t in range(count)
    ]
    others = pl.ds(0, everyone - 1)
    late[1].wait()
    late[2].wait()
    wait_bytes(norm_recv.at[others], all_recv_sem.at[0])
    columns = gather_lanes(norm_recv).astype(BF16)
    gate = jnp.dot(columns, wgate[...], preferred_element_type=F32)
    up = jnp.dot(columns, wup[...], preferred_element_type=F32)
    for c in range(req_count):
        rows = slice(c * group, (c + 1) * group)
        gate_send[c] = jnp.concatenate([gate[rows], up[rows]], axis=0).astype(BF16)

    gate_copies = req_exchange(0, lambda other: gate_send.at[other], gate_recv)
    gate_recv[req] = gate_send[req]
    wait_bytes(norm_recv.at[others], all_send_sem.at[0])
    req_arrivals(0, lambda other: gate_send.at[other], gate_recv)
    both = functools.reduce(
        lambda a, b: a + b, [gate_recv[c].astype(F32) for c in range(req_count)]
    )
    gate, up = both[:group], both[group:]
    hidden = gate / (1.0 + jnp.exp(-gate)) * up
    half = hidden.shape[1] // 2
    hid_send[...] = jnp.concatenate([hidden[:, :half], hidden[:, half:]], axis=0).astype(BF16)

    hid_copies = req_exchange(1, lambda other: hid_send, hid_recv)
    hid_recv[req] = hid_send[...]
    finish(gate_copies)
    late[3].wait()
    req_arrivals(1, lambda other: hid_send, hid_recv)
    stacked = hid_recv[...].reshape(req_count * 2 * group, half)
    first = jnp.dot(stacked, wdown[:half], preferred_element_type=F32)
    second = jnp.dot(stacked, wdown[half:], preferred_element_type=F32)
    for c in range(req_count):
        low = 2 * group * c
        part = first[low : low + group] + second[low + group : low + 2 * group]
        scatter_lanes(down_send.at[pl.ds(c * group, group)], part)

    all_exchange(1, lambda other, other_req: down_send.at[other], down_recv)
    down_recv[me] = down_send[me]
    finish(hid_copies)
    wait_bytes(down_recv.at[others], all_recv_sem.at[1])
    for c in range(req_count):
        mlp_row[c * chunk : (c + 1) * chunk] = functools.reduce(
            lambda a, b: a + b, [down_recv[c * blk_count + j] for j in range(blk_count)]
        )
    mlp_out = mlp_row[...]
    for t in range(count):
        streams[t] = mixed_state[t] + depth_ref[1, t] * mlp_out
    for k in range(streams.shape[1]):
        out_ref[0, :, k * LANES : (k + 1) * LANES] = streams[:, k, :]
    wait_bytes(down_recv.at[others], all_send_sem.at[1])


def on_device(
    hyper_state,
    lengths,
    key_cache,
    value_cache,
    attn_in_weight,
    attn_out_weight,
    w_gate,
    w_up,
    w_down,
    width_in,
    stream_mix,
    depth_out,
):
    req_count = lax.axis_size("req")
    blk_count = lax.axis_size("blk")
    everyone = req_count * blk_count
    _, count, width = hyper_state.shape
    group, _, _, head = key_cache.shape
    feature_part, hid_part = w_gate.shape
    parts = width // LANES
    chunk = feature_part // LANES
    freqs = np.exp(np.arange(head // 2) * (-2.0 * math.log(10000.0) / head))
    freqs = np.concatenate([freqs, freqs]).astype(np.float32)[None, :]
    vmem = pl.BlockSpec(memory_space=pltpu.VMEM)
    smem = pl.BlockSpec(memory_space=pltpu.SMEM)
    hbm = pl.BlockSpec(memory_space=pl.ANY)
    like = lambda x: pltpu.VMEM(x.shape, x.dtype)
    dma = pltpu.SemaphoreType.DMA
    big = [key_cache, value_cache, attn_in_weight, attn_out_weight, w_gate, w_up, w_down]
    return pl.pallas_call(
        functools.partial(layer_kernel, req_count, blk_count),
        out_shape=jax.ShapeDtypeStruct(hyper_state.shape, hyper_state.dtype),
        in_specs=[vmem, smem, vmem, smem, smem, smem] + [hbm] * len(big),
        out_specs=vmem,
        scratch_shapes=[like(x) for x in big]
        + [
            pltpu.VMEM((count, parts, LANES), F32),
            pltpu.VMEM((parts, LANES), F32),
            pltpu.VMEM((blk_count, parts, LANES), F32),
            pltpu.VMEM((blk_count, parts, LANES), F32),
            pltpu.VMEM((blk_count, parts, LANES), F32),
            pltpu.VMEM((req_count, chunk, LANES), F32),
            pltpu.VMEM((everyone, chunk, LANES), F32),
            pltpu.VMEM((req_count, 2 * group, hid_part), BF16),
            pltpu.VMEM((req_count, 2 * group, hid_part), BF16),
            pltpu.VMEM((2 * group, hid_part // 2), BF16),
            pltpu.VMEM((req_count, 2 * group, hid_part // 2), BF16),
            pltpu.VMEM((everyone, chunk, LANES), F32),
            pltpu.VMEM((everyone, chunk, LANES), F32),
            pltpu.VMEM((parts, LANES), F32),
            dma((7,)),
            dma((group,)),
            dma((group,)),
            dma((2, blk_count - 1)),
            dma((2, blk_count - 1)),
            dma((2, req_count - 1)),
            dma((2, req_count - 1)),
            dma((2,)),
            dma((2,)),
        ],
        compiler_params=pltpu.CompilerParams(
            collective_id=0, has_side_effects=True, vmem_limit_bytes=56 * 2**20
        ),
        name="layer_step",
    )(hyper_state, lengths, jnp.asarray(freqs), width_in, stream_mix, depth_out, *big)


def solution(mesh):
    placed = (
        P(("req", "blk"), None, None),
        P("req"),
        P("req", "blk", None, None),
        P("req", "blk", None, None),
        P(None, None, "blk"),
        P("blk", None),
        P("req", "blk"),
        P("req", "blk"),
        P("blk", "req"),
        P(),
        P(),
        P(),
    )
    return jax.shard_map(
        on_device,
        mesh=mesh,
        in_specs=placed,
        out_specs=P(("req", "blk"), None, None),
        check_vma=False,
    )
```

```python
import functools
import math

import jax
import jax.numpy as jnp
import numpy as np
from jax import lax
from jax.experimental import pallas as pl
from jax.experimental.pallas import tpu as pltpu
from jax.sharding import PartitionSpec as P

MESH = pl.DeviceIdType.MESH
LANES = 128
F32 = jnp.float32
BF16 = jnp.bfloat16


def split_two_pi():
    whole = 2.0 * math.pi
    one = float(np.round(whole * 2.0**8) / 2.0**8)
    two = float(np.round((whole - one) * 2.0**20) / 2.0**20)
    return one, two, whole - one - two


def sine_cosine(angles):
    one, two, three = split_two_pi()
    turns = jnp.floor(angles * (1.0 / (2.0 * math.pi)) + 0.5)
    rest = ((angles - turns * one) - turns * two) - turns * three
    return jnp.sin(rest), jnp.cos(rest)


def normalize(row):
    count = row.shape[0] * row.shape[1]
    center = row - jnp.sum(row, keepdims=True) * (1.0 / count)
    spread = jnp.sum(center * center, keepdims=True) * (1.0 / count)
    return center * lax.rsqrt(spread + 1e-05)


def gather_lanes(ref):
    return jnp.concatenate([ref[:, k, :] for k in range(ref.shape[1])], axis=1)


def scatter_lanes(ref, values):
    for k in range(ref.shape[1]):
        ref[:, k, :] = values[:, k * LANES : (k + 1) * LANES]


def wait_bytes(ref, sem):
    pltpu.make_async_copy(ref, ref, sem).wait()


def layer_kernel(
    req_count,
    blk_count,
    hyper_ref,
    lengths_ref,
    freq_ref,
    width_ref,
    mix_ref,
    depth_ref,
    keys_hbm,
    values_hbm,
    win_hbm,
    wout_hbm,
    wgate_hbm,
    wup_hbm,
    wdown_hbm,
    out_ref,
    keys,
    values,
    win,
    wout,
    wgate,
    wup,
    wdown,
    streams,
    row_send,
    row_recv,
    attn_send,
    attn_recv,
    norm_send,
    norm_recv,
    gate_send,
    gate_recv,
    hid_send,
    hid_recv,
    down_send,
    down_recv,
    mlp_row,
    load_sem,
    key_sem,
    value_sem,
    blk_send_sem,
    blk_recv_sem,
    req_send_sem,
    req_recv_sem,
    all_send_sem,
    all_recv_sem,
):
    req = lax.axis_index("req")
    blk = lax.axis_index("blk")
    everyone = req_count * blk_count
    me = req * blk_count + blk
    group, lines, head = keys.shape
    heads = win.shape[2] // head

    loads = [pltpu.make_async_copy(win_hbm.at[k], win.at[k], load_sem.at[k]) for k in range(3)]
    key_loads = [
        pltpu.make_async_copy(keys_hbm.at[r], keys.at[r], key_sem.at[r]) for r in range(group)
    ]
    value_loads = [
        pltpu.make_async_copy(values_hbm.at[r], values.at[r], value_sem.at[r])
        for r in range(group)
    ]
    late = [
        pltpu.make_async_copy(src, dst, load_sem.at[3 + i])
        for i, (src, dst) in enumerate(
            [(wout_hbm, wout), (wgate_hbm, wgate), (wup_hbm, wup), (wdown_hbm, wdown)]
        )
    ]
    barrier = pltpu.get_barrier_semaphore()

    def greet(i, carry):
        other = lax.rem(me + i, everyone)
        pl.semaphore_signal(
            barrier,
            inc=1,
            device_id=(other // blk_count, lax.rem(other, blk_count)),
            device_id_type=MESH,
        )
        return carry

    lax.fori_loop(1, everyone, greet, 0)
    for copy in loads + key_loads + value_loads + late:
        copy.start()

    for k in range(streams.shape[1]):
        streams[:, k, :] = hyper_ref[0, :, k * LANES : (k + 1) * LANES]
    count = streams.shape[0]
    state = [streams[s] for s in range(count)]
    row = functools.reduce(lambda a, b: a + b, [state[s] * width_ref[0, s] for s in range(count)])
    row_send[...] = normalize(row)

    pl.semaphore_wait(barrier, everyone - 1)

    def blk_exchange(phase, source_of, landing):
        copies = []
        for d in range(1, blk_count):
            other = lax.rem(blk + d, blk_count)
            copy = pltpu.make_async_remote_copy(
                src_ref=source_of(other),
                dst_ref=landing.at[blk],
                send_sem=blk_send_sem.at[phase, d - 1],
                recv_sem=blk_recv_sem.at[phase, d - 1],
                device_id=(req, other),
                device_id_type=MESH,
            )
            copy.start()
            copies.append(copy)
        return copies

    def blk_arrivals(phase, source_of, landing):
        for d in range(1, blk_count):
            other = lax.rem(blk + blk_count - d, blk_count)
            pltpu.make_async_remote_copy(
                src_ref=source_of(other),
                dst_ref=landing.at[other],
                send_sem=blk_send_sem.at[phase, d - 1],
                recv_sem=blk_recv_sem.at[phase, d - 1],
                device_id=(req, other),
                device_id_type=MESH,
            ).wait_recv()

    def req_exchange(phase, source_of, landing):
        copies = []
        for d in range(1, req_count):
            other = lax.rem(req + d, req_count)
            copy = pltpu.make_async_remote_copy(
                src_ref=source_of(other),
                dst_ref=landing.at[req],
                send_sem=req_send_sem.at[phase, d - 1],
                recv_sem=req_recv_sem.at[phase, d - 1],
                device_id=(other, blk),
                device_id_type=MESH,
            )
            copy.start()
            copies.append(copy)
        return copies

    def req_arrivals(phase, source_of, landing):
        for d in range(1, req_count):
            other = lax.rem(req + req_count - d, req_count)
            pltpu.make_async_remote_copy(
                src_ref=source_of(other),
                dst_ref=landing.at[other],
                send_sem=req_send_sem.at[phase, d - 1],
                recv_sem=req_recv_sem.at[phase, d - 1],
                device_id=(other, blk),
                device_id_type=MESH,
            ).wait_recv()

    def all_exchange(phase, source_of, landing):
        def send(i, carry):
            other = lax.rem(me + i, everyone)
            other_req = other // blk_count
            pltpu.make_async_remote_copy(
                src_ref=source_of(other, other_req),
                dst_ref=landing.at[me],
                send_sem=all_send_sem.at[phase],
                recv_sem=all_recv_sem.at[phase],
                device_id=(other_req, lax.rem(other, blk_count)),
                device_id_type=MESH,
            ).start()
            return carry

        lax.fori_loop(1, everyone, send, 0)

    def finish(copies):
        for copy in copies:
            copy.wait_send()

    row_copies = blk_exchange(0, lambda other: row_send, row_recv)
    row_recv[blk] = row_send[...]

    row_at = lax.broadcasted_iota(jnp.int32, (heads * group, 1), 0)
    request_at = lax.rem(row_at, group)
    lengths = jnp.zeros((heads * group, 1), jnp.int32)
    for r in range(group):
        lengths = jnp.where(request_at == r, lengths_ref[r], lengths)
    angles = lengths.astype(F32) * freq_ref[...]
    sine, cosine = sine_cosine(angles)
    lane = lax.broadcasted_iota(jnp.int32, (heads * group, head), 1)
    sine = jnp.where(lane < head // 2, -sine, sine)

    def rotate(part):
        return (part * cosine + pltpu.roll(part, head // 2, 1) * sine).astype(BF16)

    mixed_state = [
        functools.reduce(lambda a, b: a + b, [state[s] * mix_ref[0, s, t] for s in range(count)])
        for t in range(count)
    ]

    blk_arrivals(0, lambda other: row_send, row_recv)
    normed = gather_lanes(row_recv).astype(BF16)
    projected = []
    for k in range(3):
        loads[k].wait()
        projected.append(jnp.dot(normed, win[k], preferred_element_type=F32))
    finish(row_copies)

    scale = head ** (-0.5)

    def by_head(part):
        return jnp.concatenate([part[:, h * head : (h + 1) * head] for h in range(heads)], axis=0)

    query = rotate(by_head(projected[0]))
    key_new = rotate(by_head(projected[1]))
    value_new = by_head(projected[2]).astype(BF16).astype(F32)
    own = scale * jnp.sum(query.astype(F32) * key_new.astype(F32), axis=-1, keepdims=True)
    for r in range(group):
        key_loads[r].wait()
        part = lax.dot_general(
            query, keys[r], (((1,), (1,)), ((), ())), preferred_element_type=F32
        )
        scores = part if r == 0 else jnp.where(request_at == r, part, scores)
    line = lax.broadcasted_iota(jnp.int32, (heads * group, lines), 1)
    head_at = row_at // group
    valid = (line < lengths * heads) & (lax.rem(line, heads) == head_at)
    scores = jnp.where(valid, scores * scale, -jnp.inf)
    peak = jnp.maximum(jnp.max(scores, axis=-1, keepdims=True), own)
    shares = jnp.exp(scores - peak)
    own_share = jnp.exp(own - peak)
    denom = jnp.sum(shares, axis=-1, keepdims=True) + own_share
    shares = shares.astype(BF16)
    for r in range(group):
        value_loads[r].wait()
        part = jnp.dot(shares, values[r], preferred_element_type=F32)
        mixed = part if r == 0 else jnp.where(request_at == r, part, mixed)
    mixed = ((mixed + own_share * value_new) / denom).astype(BF16)
    flat = jnp.concatenate(
        [mixed[h * group : (h + 1) * group] for h in range(heads)], axis=1
    )
    late[0].wait()
    scatter_lanes(attn_send, jnp.dot(flat, wout[...], preferred_element_type=F32))

    attn_copies = blk_exchange(1, lambda other: attn_send.at[other], attn_recv)
    attn_recv[blk] = attn_send[blk]
    blk_arrivals(1, lambda other: attn_send.at[other], attn_recv)
    attn_out = functools.reduce(lambda a, b: a + b, [attn_recv[j] for j in range(blk_count)])
    state = [mixed_state[t] + depth_ref[0, t] * attn_out for t in range(count)]
    row = functools.reduce(lambda a, b: a + b, [state[s] * width_ref[1, s] for s in range(count)])
    row = normalize(row)
    chunk = norm_send.shape[1]
    for c in range(req_count):
        norm_send[c] = row[c * chunk : (c + 1) * chunk]

    all_exchange(0, lambda other, other_req: norm_send.at[other_req], norm_recv)
    norm_recv[me] = norm_send[req]
    finish(attn_copies)
    mixed_state = [
        functools.reduce(lambda a, b: a + b, [state[s] * mix_ref[1, s, t] for s in range(count)])
        for t in range(count)
    ]
    others = pl.ds(0, everyone - 1)
    late[1].wait()
    late[2].wait()
    wait_bytes(norm_recv.at[others], all_recv_sem.at[0])
    columns = gather_lanes(norm_recv).astype(BF16)
    gate = jnp.dot(columns, wgate[...], preferred_element_type=F32)
    up = jnp.dot(columns, wup[...], preferred_element_type=F32)
    for c in range(req_count):
        rows = slice(c * group, (c + 1) * group)
        gate_send[c] = jnp.concatenate([gate[rows], up[rows]], axis=0).astype(BF16)

    gate_copies = req_exchange(0, lambda other: gate_send.at[other], gate_recv)
    gate_recv[req] = gate_send[req]
    wait_bytes(norm_recv.at[others], all_send_sem.at[0])
    req_arrivals(0, lambda other: gate_send.at[other], gate_recv)
    both = functools.reduce(
        lambda a, b: a + b, [gate_recv[c].astype(F32) for c in range(req_count)]
    )
    gate, up = both[:group], both[group:]
    hidden = gate / (1.0 + jnp.exp(-gate)) * up
    half = hidden.shape[1] // 2
    hid_send[...] = jnp.concatenate([hidden[:, :half], hidden[:, half:]], axis=0).astype(BF16)

    hid_copies = req_exchange(1, lambda other: hid_send, hid_recv)
    hid_recv[req] = hid_send[...]
    finish(gate_copies)
    late[3].wait()
    req_arrivals(1, lambda other: hid_send, hid_recv)
    stacked = hid_recv[...].reshape(req_count * 2 * group, half)
    first = jnp.dot(stacked, wdown[:half], preferred_element_type=F32)
    second = jnp.dot(stacked, wdown[half:], preferred_element_type=F32)
    for c in range(req_count):
        low = 2 * group * c
        part = first[low : low + group] + second[low + group : low + 2 * group]
        scatter_lanes(down_send.at[pl.ds(c * group, group)], part)

    all_exchange(1, lambda other, other_req: down_send.at[other], down_recv)
    down_recv[me] = down_send[me]
    finish(hid_copies)
    wait_bytes(down_recv.at[others], all_recv_sem.at[1])
    for c in range(req_count):
        mlp_row[c * chunk : (c + 1) * chunk] = functools.reduce(
            lambda a, b: a + b, [down_recv[c * blk_count + j] for j in range(blk_count)]
        )
    mlp_out = mlp_row[...]
    for t in range(count):
        streams[t] = mixed_state[t] + depth_ref[1, t] * mlp_out
    for k in range(streams.shape[1]):
        out_ref[0, :, k * LANES : (k + 1) * LANES] = streams[:, k, :]
    wait_bytes(down_recv.at[others], all_send_sem.at[1])


def on_device(
    hyper_state,
    lengths,
    key_cache,
    value_cache,
    attn_in_weight,
    attn_out_weight,
    w_gate,
    w_up,
    w_down,
    width_in,
    stream_mix,
    depth_out,
):
    req_count = lax.axis_size("req")
    blk_count = lax.axis_size("blk")
    everyone = req_count * blk_count
    _, count, width = hyper_state.shape
    group, heads, slots, head = key_cache.shape
    feature_part, hid_part = w_gate.shape
    parts = width // LANES
    chunk = feature_part // LANES
    freqs = np.exp(np.arange(head // 2) * (-2.0 * math.log(10000.0) / head))
    freqs = np.concatenate([freqs, freqs]).astype(np.float32)[None, :]
    vmem = pl.BlockSpec(memory_space=pltpu.VMEM)
    smem = pl.BlockSpec(memory_space=pltpu.SMEM)
    hbm = pl.BlockSpec(memory_space=pl.ANY)
    like = lambda x: pltpu.VMEM(x.shape, x.dtype)
    dma = pltpu.SemaphoreType.DMA
    lines = lambda x: jnp.transpose(x, (0, 2, 1, 3)).reshape(group, slots * heads, head)
    big = [lines(key_cache), lines(value_cache), attn_in_weight, attn_out_weight, w_gate, w_up, w_down]
    return pl.pallas_call(
        functools.partial(layer_kernel, req_count, blk_count),
        out_shape=jax.ShapeDtypeStruct(hyper_state.shape, hyper_state.dtype),
        in_specs=[vmem, smem, vmem, smem, smem, smem] + [hbm] * len(big),
        out_specs=vmem,
        scratch_shapes=[like(x) for x in big]
        + [
            pltpu.VMEM((count, parts, LANES), F32),
            pltpu.VMEM((parts, LANES), F32),
            pltpu.VMEM((blk_count, parts, LANES), F32),
            pltpu.VMEM((blk_count, parts, LANES), F32),
            pltpu.VMEM((blk_count, parts, LANES), F32),
            pltpu.VMEM((req_count, chunk, LANES), F32),
            pltpu.VMEM((everyone, chunk, LANES), F32),
            pltpu.VMEM((req_count, 2 * group, hid_part), BF16),
            pltpu.VMEM((req_count, 2 * group, hid_part), BF16),
            pltpu.VMEM((2 * group, hid_part // 2), BF16),
            pltpu.VMEM((req_count, 2 * group, hid_part // 2), BF16),
            pltpu.VMEM((everyone, chunk, LANES), F32),
            pltpu.VMEM((everyone, chunk, LANES), F32),
            pltpu.VMEM((parts, LANES), F32),
            dma((7,)),
            dma((group,)),
            dma((group,)),
            dma((2, blk_count - 1)),
            dma((2, blk_count - 1)),
            dma((2, req_count - 1)),
            dma((2, req_count - 1)),
            dma((2,)),
            dma((2,)),
        ],
        compiler_params=pltpu.CompilerParams(
            collective_id=0, has_side_effects=True, vmem_limit_bytes=56 * 2**20
        ),
        name="layer_step",
    )(hyper_state, lengths, jnp.asarray(freqs), width_in, stream_mix, depth_out, *big)


def solution(mesh):
    placed = (
        P(("req", "blk"), None, None),
        P("req"),
        P("req", "blk", None, None),
        P("req", "blk", None, None),
        P(None, None, "blk"),
        P("blk", None),
        P("req", "blk"),
        P("req", "blk"),
        P("blk", "req"),
        P(),
        P(),
        P(),
    )
    return jax.shard_map(
        on_device,
        mesh=mesh,
        in_specs=placed,
        out_specs=P(("req", "blk"), None, None),
        check_vma=False,
    )
```

```python
import functools
import math

import jax
import jax.numpy as jnp
import numpy as np
from jax import lax
from jax.experimental import pallas as pl
from jax.experimental.pallas import tpu as pltpu
from jax.sharding import PartitionSpec as P

MESH = pl.DeviceIdType.MESH
LANES = 128
F32 = jnp.float32
BF16 = jnp.bfloat16


def split_two_pi():
    whole = 2.0 * math.pi
    one = float(np.round(whole * 2.0**8) / 2.0**8)
    two = float(np.round((whole - one) * 2.0**20) / 2.0**20)
    return one, two, whole - one - two


def sine_cosine(angles):
    one, two, three = split_two_pi()
    turns = jnp.floor(angles * (1.0 / (2.0 * math.pi)) + 0.5)
    rest = ((angles - turns * one) - turns * two) - turns * three
    return jnp.sin(rest), jnp.cos(rest)


def normalize(row):
    count = row.shape[0] * row.shape[1]
    center = row - jnp.sum(row, keepdims=True) * (1.0 / count)
    spread = jnp.sum(center * center, keepdims=True) * (1.0 / count)
    return center * lax.rsqrt(spread + 1e-05)


def gather_lanes(ref):
    return jnp.concatenate([ref[:, k, :] for k in range(ref.shape[1])], axis=1)


def scatter_lanes(ref, values):
    for k in range(ref.shape[1]):
        ref[:, k, :] = values[:, k * LANES : (k + 1) * LANES]


def wait_bytes(ref, sem):
    pltpu.make_async_copy(ref, ref, sem).wait()


def layer_kernel(
    req_count,
    blk_count,
    hyper_ref,
    lengths_ref,
    freq_ref,
    width_ref,
    mix_ref,
    depth_ref,
    keys_hbm,
    values_hbm,
    win_hbm,
    wout_hbm,
    wgate_hbm,
    wup_hbm,
    wdown_hbm,
    out_ref,
    keys,
    values,
    win,
    wout,
    wgate,
    wup,
    wdown,
    streams,
    wide_rows,
    row_send,
    row_recv,
    attn_send,
    attn_recv,
    norm_send,
    norm_recv,
    gate_send,
    gate_recv,
    up_send,
    up_recv,
    hid_send,
    hid_recv,
    down_send,
    down_recv,
    mlp_row,
    load_sem,
    key_sem,
    value_sem,
    blk_send_sem,
    blk_recv_sem,
    req_send_sem,
    req_recv_sem,
    all_send_sem,
    all_recv_sem,
):
    req = lax.axis_index("req")
    blk = lax.axis_index("blk")
    everyone = req_count * blk_count
    me = req * blk_count + blk
    group, lines, head = keys.shape
    heads = win.shape[2] // head

    loads = [pltpu.make_async_copy(win_hbm.at[k], win.at[k], load_sem.at[k]) for k in range(3)]
    key_loads = [
        pltpu.make_async_copy(keys_hbm.at[r], keys.at[r], key_sem.at[r]) for r in range(group)
    ]
    value_loads = [
        pltpu.make_async_copy(values_hbm.at[r], values.at[r], value_sem.at[r])
        for r in range(group)
    ]
    late = [
        pltpu.make_async_copy(src, dst, load_sem.at[3 + i])
        for i, (src, dst) in enumerate(
            [(wout_hbm, wout), (wgate_hbm, wgate), (wup_hbm, wup), (wdown_hbm, wdown)]
        )
    ]
    barrier = pltpu.get_barrier_semaphore()

    reqs = [req] + [lax.rem(req + d, req_count) for d in range(1, req_count)]
    blks = [blk] + [lax.rem(blk + d, blk_count) for d in range(1, blk_count)]
    peers = [
        (reqs[i], blks[j]) for i in range(req_count) for j in range(blk_count) if i + j > 0
    ]
    for copy in loads:
        copy.start()
    for peer in peers:
        pl.semaphore_signal(barrier, inc=1, device_id=peer, device_id_type=MESH)
    for copy in key_loads + value_loads + late:
        copy.start()

    for k in range(streams.shape[1]):
        streams[:, k, :] = hyper_ref[0, :, k * LANES : (k + 1) * LANES]
    count = streams.shape[0]
    state = [streams[s] for s in range(count)]
    row = functools.reduce(lambda a, b: a + b, [state[s] * width_ref[0, s] for s in range(count)])
    row_send[...] = normalize(row).astype(BF16)

    pl.semaphore_wait(barrier, everyone - 1)

    def blk_copy(phase, d, source, landing, slot, other):
        return pltpu.make_async_remote_copy(
            src_ref=source,
            dst_ref=landing.at[slot],
            send_sem=blk_send_sem.at[phase, d - 1],
            recv_sem=blk_recv_sem.at[phase, d - 1],
            device_id=(req, other),
            device_id_type=MESH,
        )

    def blk_exchange(phase, source_of, landing):
        copies = [
            blk_copy(phase, d, source_of(blks[d]), landing, blk, blks[d])
            for d in range(1, blk_count)
        ]
        for copy in copies:
            copy.start()
        return copies

    def blk_arrivals(phase, source_of, landing):
        for d in range(1, blk_count):
            other = blks[blk_count - d]
            blk_copy(phase, d, source_of(other), landing, other, other).wait_recv()

    def req_copy(phase, d, source, landing, slot, other):
        return pltpu.make_async_remote_copy(
            src_ref=source,
            dst_ref=landing.at[slot],
            send_sem=req_send_sem.at[phase, d - 1],
            recv_sem=req_recv_sem.at[phase, d - 1],
            device_id=(other, blk),
            device_id_type=MESH,
        )

    def req_exchange(phase, source_of, landing):
        copies = [
            req_copy(phase, d, source_of(reqs[d]), landing, req, reqs[d])
            for d in range(1, req_count)
        ]
        for copy in copies:
            copy.start()
        return copies

    def req_arrivals(phase, source_of, landing):
        for d in range(1, req_count):
            other = reqs[req_count - d]
            req_copy(phase, d, source_of(other), landing, other, other).wait_recv()

    def all_exchange(phase, source_of, landing):
        for peer in peers:
            pltpu.make_async_remote_copy(
                src_ref=source_of(peer),
                dst_ref=landing.at[me],
                send_sem=all_send_sem.at[phase],
                recv_sem=all_recv_sem.at[phase],
                device_id=peer,
                device_id_type=MESH,
            ).start()

    def finish(copies):
        for copy in copies:
            copy.wait_send()

    row_copies = blk_exchange(0, lambda other: row_send, row_recv)
    row_recv[blk] = row_send[...]

    row_at = lax.broadcasted_iota(jnp.int32, (heads * group, 1), 0)
    request_at = lax.rem(row_at, group)
    lengths = jnp.zeros((heads * group, 1), jnp.int32)
    for r in range(group):
        lengths = jnp.where(request_at == r, lengths_ref[r], lengths)
    angles = lengths.astype(F32) * freq_ref[...]
    sine, cosine = sine_cosine(angles)
    lane = lax.broadcasted_iota(jnp.int32, (heads * group, head), 1)
    sine = jnp.where(lane < head // 2, -sine, sine)

    def rotate(part):
        return (part * cosine + pltpu.roll(part, head // 2, 1) * sine).astype(BF16)

    mixed_state = [
        functools.reduce(lambda a, b: a + b, [state[s] * mix_ref[0, s, t] for s in range(count)])
        for t in range(count)
    ]

    blk_arrivals(0, lambda other: row_send, row_recv)
    wide_rows[...] = row_recv[...].astype(F32)
    normed = gather_lanes(wide_rows).astype(BF16)
    projected = []
    for k in range(3):
        loads[k].wait()
        projected.append(jnp.dot(normed, win[k], preferred_element_type=F32))
    finish(row_copies)

    scale = head ** (-0.5)

    def by_head(part):
        return jnp.concatenate([part[:, h * head : (h + 1) * head] for h in range(heads)], axis=0)

    query = rotate(by_head(projected[0]))
    key_new = rotate(by_head(projected[1]))
    value_new = by_head(projected[2]).astype(BF16).astype(F32)
    own = scale * jnp.sum(query.astype(F32) * key_new.astype(F32), axis=-1, keepdims=True)
    for r in range(group):
        key_loads[r].wait()
        part = lax.dot_general(
            query, keys[r], (((1,), (1,)), ((), ())), preferred_element_type=F32
        )
        scores = part if r == 0 else jnp.where(request_at == r, part, scores)
    line = lax.broadcasted_iota(jnp.int32, (heads * group, lines), 1)
    head_at = row_at // group
    valid = (line < lengths * heads) & (lax.rem(line, heads) == head_at)
    scores = jnp.where(valid, scores * scale, -jnp.inf)
    peak = jnp.maximum(jnp.max(scores, axis=-1, keepdims=True), own)
    shares = jnp.exp(scores - peak)
    own_share = jnp.exp(own - peak)
    denom = jnp.sum(shares, axis=-1, keepdims=True) + own_share
    shares = shares.astype(BF16)
    for r in range(group):
        value_loads[r].wait()
        part = jnp.dot(shares, values[r], preferred_element_type=F32)
        mixed = part if r == 0 else jnp.where(request_at == r, part, mixed)
    mixed = ((mixed + own_share * value_new) / denom).astype(BF16)
    flat = jnp.concatenate(
        [mixed[h * group : (h + 1) * group] for h in range(heads)], axis=1
    )
    late[0].wait()
    scatter_lanes(wide_rows, jnp.dot(flat, wout[...], preferred_element_type=F32))
    attn_send[...] = wide_rows[...].astype(BF16)

    attn_copies = blk_exchange(1, lambda other: attn_send.at[other], attn_recv)
    attn_recv[blk] = attn_send[blk]
    blk_arrivals(1, lambda other: attn_send.at[other], attn_recv)
    attn_out = functools.reduce(lambda a, b: a + b, [attn_recv[j].astype(F32) for j in range(blk_count)])
    state = [mixed_state[t] + depth_ref[0, t] * attn_out for t in range(count)]
    row = functools.reduce(lambda a, b: a + b, [state[s] * width_ref[1, s] for s in range(count)])
    row = normalize(row)
    chunk = norm_send.shape[1]
    for c in range(req_count):
        norm_send[c] = row[c * chunk : (c + 1) * chunk]

    all_exchange(0, lambda peer: norm_send.at[peer[0]], norm_recv)
    norm_recv[me] = norm_send[req]
    finish(attn_copies)
    mixed_state = [
        functools.reduce(lambda a, b: a + b, [state[s] * mix_ref[1, s, t] for s in range(count)])
        for t in range(count)
    ]
    others = pl.ds(0, everyone - 1)
    late[1].wait()
    late[2].wait()
    wait_bytes(norm_recv.at[others], all_recv_sem.at[0])
    columns = gather_lanes(norm_recv).astype(BF16)
    half = wgate.shape[1] // 2

    def spread(part, landing):
        for c in range(req_count):
            rows = slice(c * group, (c + 1) * group)
            landing[c] = jnp.concatenate([part[rows, :half], part[rows, half:]], axis=0).astype(
                BF16
            )

    def total(landing):
        return functools.reduce(
            lambda a, b: a + b, [landing[c].astype(F32) for c in range(req_count)]
        )

    spread(jnp.dot(columns, wgate[...], preferred_element_type=F32), gate_send)
    gate_copies = req_exchange(0, lambda other: gate_send.at[other], gate_recv)
    spread(jnp.dot(columns, wup[...], preferred_element_type=F32), up_send)
    gate_copies += req_exchange(1, lambda other: up_send.at[other], up_recv)
    gate_recv[req] = gate_send[req]
    up_recv[req] = up_send[req]
    wait_bytes(norm_recv.at[others], all_send_sem.at[0])
    req_arrivals(0, lambda other: gate_send.at[other], gate_recv)
    gate = total(gate_recv)
    gate = gate / (1.0 + jnp.exp(-gate))
    req_arrivals(1, lambda other: up_send.at[other], up_recv)
    hid_send[...] = (gate * total(up_recv)).astype(BF16)

    hid_copies = req_exchange(2, lambda other: hid_send, hid_recv)
    hid_recv[req] = hid_send[...]
    finish(gate_copies)
    late[3].wait()
    req_arrivals(2, lambda other: hid_send, hid_recv)
    stacked = hid_recv[...].reshape(req_count * 2 * group, half)
    first = jnp.dot(stacked, wdown[:half], preferred_element_type=F32)
    second = jnp.dot(stacked, wdown[half:], preferred_element_type=F32)
    for c in range(req_count):
        low = 2 * group * c
        part = first[low : low + group] + second[low + group : low + 2 * group]
        scatter_lanes(down_send.at[pl.ds(c * group, group)], part)

    all_exchange(1, lambda peer: down_send.at[peer[0] * blk_count + peer[1]], down_recv)
    down_recv[me] = down_send[me]
    finish(hid_copies)
    wait_bytes(down_recv.at[others], all_recv_sem.at[1])
    for c in range(req_count):
        mlp_row[c * chunk : (c + 1) * chunk] = functools.reduce(
            lambda a, b: a + b, [down_recv[c * blk_count + j] for j in range(blk_count)]
        )
    mlp_out = mlp_row[...]
    for t in range(count):
        out_ref[0, t] = mixed_state[t] + depth_ref[1, t] * mlp_out
    wait_bytes(down_recv.at[others], all_send_sem.at[1])


def on_device(
    hyper_state,
    lengths,
    key_cache,
    value_cache,
    attn_in_weight,
    attn_out_weight,
    w_gate,
    w_up,
    w_down,
    width_in,
    stream_mix,
    depth_out,
):
    req_count = lax.axis_size("req")
    blk_count = lax.axis_size("blk")
    everyone = req_count * blk_count
    _, count, width = hyper_state.shape
    group, heads, slots, head = key_cache.shape
    feature_part, hid_part = w_gate.shape
    parts = width // LANES
    chunk = feature_part // LANES
    freqs = np.exp(np.arange(head // 2) * (-2.0 * math.log(10000.0) / head))
    freqs = np.concatenate([freqs, freqs]).astype(np.float32)[None, :]
    vmem = pl.BlockSpec(memory_space=pltpu.VMEM)
    smem = pl.BlockSpec(memory_space=pltpu.SMEM)
    hbm = pl.BlockSpec(memory_space=pl.ANY)
    like = lambda x: pltpu.VMEM(x.shape, x.dtype)
    dma = pltpu.SemaphoreType.DMA
    lines = lambda x: jnp.transpose(x, (0, 2, 1, 3)).reshape(group, slots * heads, head)
    big = [lines(key_cache), lines(value_cache), attn_in_weight, attn_out_weight, w_gate, w_up, w_down]
    return pl.pallas_call(
        functools.partial(layer_kernel, req_count, blk_count),
        out_shape=jax.ShapeDtypeStruct((1, count, parts, LANES), F32),
        in_specs=[vmem, smem, vmem, smem, smem, smem] + [hbm] * len(big),
        out_specs=vmem,
        scratch_shapes=[like(x) for x in big]
        + [
            pltpu.VMEM((count, parts, LANES), F32),
            pltpu.VMEM((blk_count, parts, LANES), F32),
            pltpu.VMEM((parts, LANES), BF16),
            pltpu.VMEM((blk_count, parts, LANES), BF16),
            pltpu.VMEM((blk_count, parts, LANES), BF16),
            pltpu.VMEM((blk_count, parts, LANES), BF16),
            pltpu.VMEM((req_count, chunk, LANES), F32),
            pltpu.VMEM((everyone, chunk, LANES), F32),
            pltpu.VMEM((req_count, 2 * group, hid_part // 2), BF16),
            pltpu.VMEM((req_count, 2 * group, hid_part // 2), BF16),
            pltpu.VMEM((req_count, 2 * group, hid_part // 2), BF16),
            pltpu.VMEM((req_count, 2 * group, hid_part // 2), BF16),
            pltpu.VMEM((2 * group, hid_part // 2), BF16),
            pltpu.VMEM((req_count, 2 * group, hid_part // 2), BF16),
            pltpu.VMEM((everyone, chunk, LANES), F32),
            pltpu.VMEM((everyone, chunk, LANES), F32),
            pltpu.VMEM((parts, LANES), F32),
            dma((7,)),
            dma((group,)),
            dma((group,)),
            dma((2, blk_count - 1)),
            dma((2, blk_count - 1)),
            dma((3, req_count - 1)),
            dma((3, req_count - 1)),
            dma((2,)),
            dma((2,)),
        ],
        compiler_params=pltpu.CompilerParams(
            collective_id=0, has_side_effects=True, vmem_limit_bytes=56 * 2**20
        ),
        name="layer_step",
    )(hyper_state, lengths, jnp.asarray(freqs), width_in, stream_mix, depth_out, *big).reshape(hyper_state.shape)


def solution(mesh):
    placed = (
        P(("req", "blk"), None, None),
        P("req"),
        P("req", "blk", None, None),
        P("req", "blk", None, None),
        P(None, None, "blk"),
        P("blk", None),
        P("req", "blk"),
        P("req", "blk"),
        P("blk", "req"),
        P(),
        P(),
        P(),
    )
    return jax.shard_map(
        on_device,
        mesh=mesh,
        in_specs=placed,
        out_specs=P(("req", "blk"), None, None),
        check_vma=False,
    )
```

```python
import functools
import math

import jax
import jax.numpy as jnp
import numpy as np
from jax import lax
from jax.experimental import pallas as pl
from jax.experimental.pallas import tpu as pltpu
from jax.sharding import PartitionSpec as P

MESH = pl.DeviceIdType.MESH
LANES = 128
F32 = jnp.float32
BF16 = jnp.bfloat16


def split_two_pi():
    whole = 2.0 * math.pi
    one = float(np.round(whole * 2.0**8) / 2.0**8)
    two = float(np.round((whole - one) * 2.0**20) / 2.0**20)
    return one, two, whole - one - two


def sine_cosine(angles):
    one, two, three = split_two_pi()
    turns = jnp.floor(angles * (1.0 / (2.0 * math.pi)) + 0.5)
    rest = ((angles - turns * one) - turns * two) - turns * three
    return jnp.sin(rest), jnp.cos(rest)


def normalize(row):
    count = row.shape[0] * row.shape[1]
    center = row - jnp.sum(row, keepdims=True) * (1.0 / count)
    spread = jnp.sum(center * center, keepdims=True) * (1.0 / count)
    return center * lax.rsqrt(spread + 1e-05)


def gather_lanes(ref):
    return jnp.concatenate([ref[:, k, :] for k in range(ref.shape[1])], axis=1)


def scatter_lanes(ref, values):
    for k in range(ref.shape[1]):
        ref[:, k, :] = values[:, k * LANES : (k + 1) * LANES]


def wait_bytes(ref, sem):
    pltpu.make_async_copy(ref, ref, sem).wait()


def layer_kernel(
    req_count,
    blk_count,
    hyper_hbm,
    lengths_hbm,
    freq_hbm,
    width_hbm,
    mix_hbm,
    depth_hbm,
    keys_hbm,
    values_hbm,
    win_hbm,
    wout_hbm,
    wgate_hbm,
    wup_hbm,
    wdown_hbm,
    out_ref,
    hyper_ref,
    lengths_ref,
    freq_ref,
    width_ref,
    mix_ref,
    depth_ref,
    bias,
    keys,
    values,
    win,
    wout,
    wgate,
    wup,
    wdown,
    streams,
    wide_rows,
    row_send,
    row_recv,
    attn_send,
    attn_recv,
    norm_send,
    norm_recv,
    gate_send,
    gate_recv,
    up_send,
    up_recv,
    hid_send,
    hid_recv,
    down_send,
    down_recv,
    mlp_row,
    small_sem,
    load_sem,
    key_sem,
    value_sem,
    blk_send_sem,
    blk_recv_sem,
    req_send_sem,
    req_recv_sem,
    all_send_sem,
    all_recv_sem,
):
    req = lax.axis_index("req")
    blk = lax.axis_index("blk")
    everyone = req_count * blk_count
    me = req * blk_count + blk
    group, lines, head = keys.shape
    heads = win.shape[2] // head

    small = [
        pltpu.make_async_copy(src, dst, small_sem.at[i])
        for i, (src, dst) in enumerate(
            [
                (hyper_hbm, hyper_ref),
                (width_hbm, width_ref),
                (lengths_hbm, lengths_ref),
                (freq_hbm, freq_ref),
                (mix_hbm, mix_ref),
                (depth_hbm, depth_ref),
            ]
        )
    ]
    loads = [pltpu.make_async_copy(win_hbm.at[k], win.at[k], load_sem.at[k]) for k in range(3)]
    key_loads = [
        pltpu.make_async_copy(keys_hbm.at[r], keys.at[r], key_sem.at[r]) for r in range(group)
    ]
    value_loads = [
        pltpu.make_async_copy(values_hbm.at[r], values.at[r], value_sem.at[r])
        for r in range(group)
    ]
    late = [
        pltpu.make_async_copy(src, dst, load_sem.at[3 + i])
        for i, (src, dst) in enumerate(
            [(wout_hbm, wout), (wgate_hbm, wgate), (wup_hbm, wup), (wdown_hbm, wdown)]
        )
    ]
    barrier = pltpu.get_barrier_semaphore()

    reqs = [req] + [lax.rem(req + d, req_count) for d in range(1, req_count)]
    blks = [blk] + [lax.rem(blk + d, blk_count) for d in range(1, blk_count)]
    peers = [
        (reqs[i], blks[j]) for i in range(req_count) for j in range(blk_count) if i + j > 0
    ]
    for copy in small + loads:
        copy.start()
    for peer in peers:
        pl.semaphore_signal(barrier, inc=1, device_id=peer, device_id_type=MESH)
    for copy in key_loads + value_loads + late:
        copy.start()

    for copy in small:
        copy.wait()

    for k in range(streams.shape[1]):
        streams[:, k, :] = hyper_ref[0, :, k * LANES : (k + 1) * LANES]
    count = streams.shape[0]
    state = [streams[s] for s in range(count)]
    row = functools.reduce(lambda a, b: a + b, [state[s] * width_ref[0, s] for s in range(count)])
    row_send[...] = normalize(row).astype(BF16)

    pl.semaphore_wait(barrier, everyone - 1)

    def blk_copy(phase, d, source, landing, slot, other):
        return pltpu.make_async_remote_copy(
            src_ref=source,
            dst_ref=landing.at[slot],
            send_sem=blk_send_sem.at[phase, d - 1],
            recv_sem=blk_recv_sem.at[phase, d - 1],
            device_id=(req, other),
            device_id_type=MESH,
        )

    def blk_exchange(phase, source_of, landing):
        copies = [
            blk_copy(phase, d, source_of(blks[d]), landing, blk, blks[d])
            for d in range(1, blk_count)
        ]
        for copy in copies:
            copy.start()
        return copies

    def blk_arrivals(phase, source_of, landing):
        for d in range(1, blk_count):
            other = blks[blk_count - d]
            blk_copy(phase, d, source_of(other), landing, other, other).wait_recv()

    def req_copy(phase, d, source, landing, slot, other):
        return pltpu.make_async_remote_copy(
            src_ref=source,
            dst_ref=landing.at[slot],
            send_sem=req_send_sem.at[phase, d - 1],
            recv_sem=req_recv_sem.at[phase, d - 1],
            device_id=(other, blk),
            device_id_type=MESH,
        )

    def req_exchange(phase, source_of, landing):
        copies = [
            req_copy(phase, d, source_of(reqs[d]), landing, req, reqs[d])
            for d in range(1, req_count)
        ]
        for copy in copies:
            copy.start()
        return copies

    def req_arrivals(phase, source_of, landing):
        for d in range(1, req_count):
            other = reqs[req_count - d]
            req_copy(phase, d, source_of(other), landing, other, other).wait_recv()

    def all_exchange(phase, source_of, landing):
        for peer in peers:
            pltpu.make_async_remote_copy(
                src_ref=source_of(peer),
                dst_ref=landing.at[me],
                send_sem=all_send_sem.at[phase],
                recv_sem=all_recv_sem.at[phase],
                device_id=peer,
                device_id_type=MESH,
            ).start()

    def finish(copies):
        for copy in copies:
            copy.wait_send()

    row_copies = blk_exchange(0, lambda other: row_send, row_recv)
    row_recv[blk] = row_send[...]

    def rotate(part):
        return (part * cosine + pltpu.roll(part, head // 2, 1) * sine).astype(BF16)

    mixed_state = [
        functools.reduce(lambda a, b: a + b, [state[s] * mix_ref[0, s, t] for s in range(count)])
        for t in range(count)
    ]

    row_at = lax.broadcasted_iota(jnp.int32, (heads * group, 1), 0)
    request_at = lax.rem(row_at, group)
    lengths = jnp.zeros((heads * group, 1), jnp.int32)
    for r in range(group):
        lengths = jnp.where(request_at == r, lengths_ref[r], lengths)
    angles = lengths.astype(F32) * freq_ref[...]
    sine, cosine = sine_cosine(angles)
    lane = lax.broadcasted_iota(jnp.int32, (heads * group, head), 1)
    sine = jnp.where(lane < head // 2, -sine, sine)

    line = lax.broadcasted_iota(jnp.int32, (heads * group, lines), 1)
    slot = line // heads
    valid = (slot < lengths) & (line - slot * heads == row_at // group)
    bias[...] = jnp.where(valid, 0.0, -jnp.inf)

    blk_arrivals(0, lambda other: row_send, row_recv)
    wide_rows[...] = row_recv[...].astype(F32)
    normed = gather_lanes(wide_rows).astype(BF16)
    projected = []
    for k in range(3):
        loads[k].wait()
        projected.append(jnp.dot(normed, win[k], preferred_element_type=F32))
    finish(row_copies)

    scale = head ** (-0.5)

    def by_head(part):
        return jnp.concatenate([part[:, h * head : (h + 1) * head] for h in range(heads)], axis=0)

    query = rotate(by_head(projected[0]))
    key_new = rotate(by_head(projected[1]))
    value_new = by_head(projected[2]).astype(BF16).astype(F32)
    wide_query = query.astype(F32)
    own = scale * jnp.sum(wide_query * key_new.astype(F32), axis=-1, keepdims=True)
    scores = None
    for r in range(0, group, 2):
        key_loads[r].wait()
        key_loads[r + 1].wait()
        pair = jnp.concatenate(
            [jnp.where(request_at == r + i, wide_query, 0.0) for i in range(2)], axis=1
        ).astype(BF16)
        part = lax.dot_general(
            pair,
            jnp.concatenate([keys[r], keys[r + 1]], axis=1),
            (((1,), (1,)), ((), ())),
            preferred_element_type=F32,
        )
        scores = part if r == 0 else scores + part
    scores = scores * scale + bias[...]
    peak = jnp.maximum(jnp.max(scores, axis=-1, keepdims=True), own)
    shares = jnp.exp(scores - peak)
    own_share = jnp.exp(own - peak)
    denom = jnp.sum(shares, axis=-1, keepdims=True) + own_share
    shares = shares.astype(BF16)
    mixed = own_share * value_new
    for r in range(0, group, 2):
        value_loads[r].wait()
        value_loads[r + 1].wait()
        part = jnp.dot(
            shares,
            jnp.concatenate([values[r], values[r + 1]], axis=1),
            preferred_element_type=F32,
        )
        for i in range(2):
            mixed = mixed + jnp.where(
                request_at == r + i, part[:, i * head : (i + 1) * head], 0.0
            )
    mixed = (mixed / denom).astype(BF16)
    flat = jnp.concatenate(
        [mixed[h * group : (h + 1) * group] for h in range(heads)], axis=1
    )
    late[0].wait()
    scatter_lanes(wide_rows, jnp.dot(flat, wout[...], preferred_element_type=F32))
    attn_send[...] = wide_rows[...].astype(BF16)

    attn_copies = blk_exchange(1, lambda other: attn_send.at[other], attn_recv)
    attn_recv[blk] = attn_send[blk]
    blk_arrivals(1, lambda other: attn_send.at[other], attn_recv)
    attn_out = functools.reduce(lambda a, b: a + b, [attn_recv[j].astype(F32) for j in range(blk_count)])
    state = [mixed_state[t] + depth_ref[0, t] * attn_out for t in range(count)]
    row = functools.reduce(lambda a, b: a + b, [state[s] * width_ref[1, s] for s in range(count)])
    row = normalize(row)
    chunk = norm_send.shape[1]
    for c in range(req_count):
        norm_send[c] = row[c * chunk : (c + 1) * chunk]

    all_exchange(0, lambda peer: norm_send.at[peer[0]], norm_recv)
    norm_recv[me] = norm_send[req]
    finish(attn_copies)
    mixed_state = [
        functools.reduce(lambda a, b: a + b, [state[s] * mix_ref[1, s, t] for s in range(count)])
        for t in range(count)
    ]
    others = pl.ds(0, everyone - 1)
    late[1].wait()
    late[2].wait()
    wait_bytes(norm_recv.at[others], all_recv_sem.at[0])
    columns = gather_lanes(norm_recv).astype(BF16)
    half = wgate.shape[1] // 2

    def spread(part, landing):
        for c in range(req_count):
            rows = slice(c * group, (c + 1) * group)
            landing[c] = jnp.concatenate([part[rows, :half], part[rows, half:]], axis=0).astype(
                BF16
            )

    def total(landing):
        return functools.reduce(
            lambda a, b: a + b, [landing[c].astype(F32) for c in range(req_count)]
        )

    spread(jnp.dot(columns, wgate[...], preferred_element_type=F32), gate_send)
    gate_copies = req_exchange(0, lambda other: gate_send.at[other], gate_recv)
    spread(jnp.dot(columns, wup[...], preferred_element_type=F32), up_send)
    gate_copies += req_exchange(1, lambda other: up_send.at[other], up_recv)
    gate_recv[req] = gate_send[req]
    up_recv[req] = up_send[req]
    wait_bytes(norm_recv.at[others], all_send_sem.at[0])
    req_arrivals(0, lambda other: gate_send.at[other], gate_recv)
    gate = total(gate_recv)
    gate = gate / (1.0 + jnp.exp(-gate))
    req_arrivals(1, lambda other: up_send.at[other], up_recv)
    hid_send[...] = (gate * total(up_recv)).astype(BF16)

    hid_copies = req_exchange(2, lambda other: hid_send, hid_recv)
    hid_recv[req] = hid_send[...]
    finish(gate_copies)
    late[3].wait()
    req_arrivals(2, lambda other: hid_send, hid_recv)
    stacked = hid_recv[...].reshape(req_count * 2 * group, half)
    first = jnp.dot(stacked, wdown[:half], preferred_element_type=F32)
    second = jnp.dot(stacked, wdown[half:], preferred_element_type=F32)
    for c in range(req_count):
        low = 2 * group * c
        part = first[low : low + group] + second[low + group : low + 2 * group]
        scatter_lanes(down_send.at[pl.ds(c * group, group)], part)

    all_exchange(1, lambda peer: down_send.at[peer[0] * blk_count + peer[1]], down_recv)
    down_recv[me] = down_send[me]
    finish(hid_copies)
    wait_bytes(down_recv.at[others], all_recv_sem.at[1])
    for c in range(req_count):
        mlp_row[c * chunk : (c + 1) * chunk] = functools.reduce(
            lambda a, b: a + b, [down_recv[c * blk_count + j] for j in range(blk_count)]
        )
    mlp_out = mlp_row[...]
    for t in range(count):
        out_ref[0, t] = mixed_state[t] + depth_ref[1, t] * mlp_out
    wait_bytes(down_recv.at[others], all_send_sem.at[1])


def on_device(
    hyper_state,
    lengths,
    key_cache,
    value_cache,
    attn_in_weight,
    attn_out_weight,
    w_gate,
    w_up,
    w_down,
    width_in,
    stream_mix,
    depth_out,
):
    req_count = lax.axis_size("req")
    blk_count = lax.axis_size("blk")
    everyone = req_count * blk_count
    _, count, width = hyper_state.shape
    group, heads, slots, head = key_cache.shape
    feature_part, hid_part = w_gate.shape
    parts = width // LANES
    chunk = feature_part // LANES
    freqs = np.exp(np.arange(head // 2) * (-2.0 * math.log(10000.0) / head))
    freqs = np.concatenate([freqs, freqs]).astype(np.float32)[None, :]
    vmem = pl.BlockSpec(memory_space=pltpu.VMEM)
    hbm = pl.BlockSpec(memory_space=pl.ANY)
    like = lambda x: pltpu.VMEM(x.shape, x.dtype)
    scalars = lambda x: pltpu.SMEM(x.shape, x.dtype)
    dma = pltpu.SemaphoreType.DMA
    lines = lambda x: jnp.transpose(x, (0, 2, 1, 3)).reshape(group, slots * heads, head)
    big = [lines(key_cache), lines(value_cache), attn_in_weight, attn_out_weight, w_gate, w_up, w_down]
    return pl.pallas_call(
        functools.partial(layer_kernel, req_count, blk_count),
        out_shape=jax.ShapeDtypeStruct((1, count, parts, LANES), F32),
        in_specs=[hbm] * (6 + len(big)),
        out_specs=vmem,
        scratch_shapes=[
            like(hyper_state),
            scalars(lengths),
            pltpu.VMEM(freqs.shape, F32),
            scalars(width_in),
            scalars(stream_mix),
            scalars(depth_out),
            pltpu.VMEM((heads * group, slots * heads), F32),
        ]
        + [like(x) for x in big]
        + [
            pltpu.VMEM((count, parts, LANES), F32),
            pltpu.VMEM((blk_count, parts, LANES), F32),
            pltpu.VMEM((parts, LANES), BF16),
            pltpu.VMEM((blk_count, parts, LANES), BF16),
            pltpu.VMEM((blk_count, parts, LANES), BF16),
            pltpu.VMEM((blk_count, parts, LANES), BF16),
            pltpu.VMEM((req_count, chunk, LANES), F32),
            pltpu.VMEM((everyone, chunk, LANES), F32),
            pltpu.VMEM((req_count, 2 * group, hid_part // 2), BF16),
            pltpu.VMEM((req_count, 2 * group, hid_part // 2), BF16),
            pltpu.VMEM((req_count, 2 * group, hid_part // 2), BF16),
            pltpu.VMEM((req_count, 2 * group, hid_part // 2), BF16),
            pltpu.VMEM((2 * group, hid_part // 2), BF16),
            pltpu.VMEM((req_count, 2 * group, hid_part // 2), BF16),
            pltpu.VMEM((everyone, chunk, LANES), F32),
            pltpu.VMEM((everyone, chunk, LANES), F32),
            pltpu.VMEM((parts, LANES), F32),
            dma((6,)),
            dma((7,)),
            dma((group,)),
            dma((group,)),
            dma((2, blk_count - 1)),
            dma((2, blk_count - 1)),
            dma((3, req_count - 1)),
            dma((3, req_count - 1)),
            dma((2,)),
            dma((2,)),
        ],
        compiler_params=pltpu.CompilerParams(
            collective_id=0, has_side_effects=True, vmem_limit_bytes=56 * 2**20
        ),
        name="layer_step",
    )(hyper_state, lengths, jnp.asarray(freqs), width_in, stream_mix, depth_out, *big).reshape(hyper_state.shape)


def solution(mesh):
    placed = (
        P(("req", "blk"), None, None),
        P("req"),
        P("req", "blk", None, None),
        P("req", "blk", None, None),
        P(None, None, "blk"),
        P("blk", None),
        P("req", "blk"),
        P("req", "blk"),
        P("blk", "req"),
        P(),
        P(),
        P(),
    )
    return jax.shard_map(
        on_device,
        mesh=mesh,
        in_specs=placed,
        out_specs=P(("req", "blk"), None, None),
        check_vma=False,
    )
```

```python
import functools
import math

import jax
import jax.numpy as jnp
import numpy as np
from jax import lax
from jax.experimental import pallas as pl
from jax.experimental.pallas import tpu as pltpu
from jax.sharding import PartitionSpec as P

MESH = pl.DeviceIdType.MESH
LANES = 128
F32 = jnp.float32
BF16 = jnp.bfloat16


def split_two_pi():
    whole = 2.0 * math.pi
    one = float(np.round(whole * 2.0**8) / 2.0**8)
    two = float(np.round((whole - one) * 2.0**20) / 2.0**20)
    return one, two, whole - one - two


def sine_cosine(angles):
    one, two, three = split_two_pi()
    turns = jnp.floor(angles * (1.0 / (2.0 * math.pi)) + 0.5)
    rest = ((angles - turns * one) - turns * two) - turns * three
    return jnp.sin(rest), jnp.cos(rest)


def normalize(row):
    count = row.shape[0] * row.shape[1]
    center = row - jnp.sum(row, keepdims=True) * (1.0 / count)
    spread = jnp.sum(center * center, keepdims=True) * (1.0 / count)
    return center * lax.rsqrt(spread + 1e-05)


def gather_lanes(ref):
    return jnp.concatenate([ref[:, k, :] for k in range(ref.shape[1])], axis=1)


def scatter_lanes(ref, values):
    for k in range(ref.shape[1]):
        ref[:, k, :] = values[:, k * LANES : (k + 1) * LANES]


def layer_kernel(
    req_count,
    blk_count,
    hyper_hbm,
    lengths_hbm,
    freq_hbm,
    width_hbm,
    mix_hbm,
    depth_hbm,
    keys_hbm,
    values_hbm,
    win_hbm,
    wout_hbm,
    wgate_hbm,
    wup_hbm,
    wdown_hbm,
    out_ref,
    hyper_ref,
    lengths_ref,
    freq_ref,
    width_ref,
    mix_ref,
    depth_ref,
    bias,
    keys,
    values,
    win,
    wout,
    wgate,
    wup,
    wdown,
    streams,
    wide_rows,
    row_send,
    row_recv,
    attn_send,
    attn_recv,
    norm_send,
    norm_recv,
    gate_send,
    gate_recv,
    up_send,
    up_recv,
    hid_send,
    hid_recv,
    down_send,
    down_recv,
    part_send,
    part_recv,
    last_send,
    last_recv,
    joined,
    small_sem,
    load_sem,
    key_sem,
    value_sem,
    blk_send_sem,
    blk_recv_sem,
    req_send_sem,
    req_recv_sem,
):
    req = lax.axis_index("req")
    blk = lax.axis_index("blk")
    group, lines, head = keys.shape
    heads = win.shape[2] // head

    small = [
        pltpu.make_async_copy(src, dst, small_sem.at[i])
        for i, (src, dst) in enumerate(
            [
                (hyper_hbm, hyper_ref),
                (width_hbm, width_ref),
                (lengths_hbm, lengths_ref),
                (freq_hbm, freq_ref),
                (mix_hbm, mix_ref),
                (depth_hbm, depth_ref),
            ]
        )
    ]
    loads = [pltpu.make_async_copy(win_hbm.at[k], win.at[k], load_sem.at[k]) for k in range(3)]
    key_loads = [
        pltpu.make_async_copy(keys_hbm.at[r], keys.at[r], key_sem.at[r]) for r in range(group)
    ]
    value_loads = [
        pltpu.make_async_copy(values_hbm.at[r], values.at[r], value_sem.at[r])
        for r in range(group)
    ]
    late = [
        pltpu.make_async_copy(src, dst, load_sem.at[3 + i])
        for i, (src, dst) in enumerate(
            [(wout_hbm, wout), (wgate_hbm, wgate), (wup_hbm, wup), (wdown_hbm, wdown)]
        )
    ]
    barrier = pltpu.get_barrier_semaphore()

    reqs = [req] + [lax.rem(req + d, req_count) for d in range(1, req_count)]
    blks = [blk] + [lax.rem(blk + d, blk_count) for d in range(1, blk_count)]
    peers = [(req, other) for other in blks[1:]] + [(other, blk) for other in reqs[1:]]
    for copy in small + loads:
        copy.start()
    for peer in peers:
        pl.semaphore_signal(barrier, inc=1, device_id=peer, device_id_type=MESH)
    for copy in key_loads + value_loads + late:
        copy.start()

    for copy in small:
        copy.wait()

    for k in range(streams.shape[1]):
        streams[:, k, :] = hyper_ref[0, :, k * LANES : (k + 1) * LANES]
    count = streams.shape[0]
    state = [streams[s] for s in range(count)]
    row = functools.reduce(lambda a, b: a + b, [state[s] * width_ref[0, s] for s in range(count)])
    row_send[...] = normalize(row).astype(BF16)

    pl.semaphore_wait(barrier, len(peers))

    def blk_copy(phase, d, source, landing, slot, other):
        return pltpu.make_async_remote_copy(
            src_ref=source,
            dst_ref=landing.at[slot],
            send_sem=blk_send_sem.at[phase, d - 1],
            recv_sem=blk_recv_sem.at[phase, d - 1],
            device_id=(req, other),
            device_id_type=MESH,
        )

    def blk_exchange(phase, source_of, landing):
        copies = [
            blk_copy(phase, d, source_of(blks[d]), landing, blk, blks[d])
            for d in range(1, blk_count)
        ]
        for copy in copies:
            copy.start()
        return copies

    def blk_arrivals(phase, source_of, landing):
        for d in range(1, blk_count):
            other = blks[blk_count - d]
            blk_copy(phase, d, source_of(other), landing, other, other).wait_recv()

    def req_copy(phase, d, source, landing, slot, other):
        return pltpu.make_async_remote_copy(
            src_ref=source,
            dst_ref=landing.at[slot],
            send_sem=req_send_sem.at[phase, d - 1],
            recv_sem=req_recv_sem.at[phase, d - 1],
            device_id=(other, blk),
            device_id_type=MESH,
        )

    def req_exchange(phase, source_of, landing):
        copies = [
            req_copy(phase, d, source_of(reqs[d]), landing, req, reqs[d])
            for d in range(1, req_count)
        ]
        for copy in copies:
            copy.start()
        return copies

    def req_arrivals(phase, source_of, landing):
        for d in range(1, req_count):
            other = reqs[req_count - d]
            req_copy(phase, d, source_of(other), landing, other, other).wait_recv()

    def finish(copies):
        for copy in copies:
            copy.wait_send()

    row_copies = blk_exchange(0, lambda other: row_send, row_recv)
    row_recv[blk] = row_send[...]

    def rotate(part):
        return (part * cosine + pltpu.roll(part, head // 2, 1) * sine).astype(BF16)

    mixed_state = [
        functools.reduce(lambda a, b: a + b, [state[s] * mix_ref[0, s, t] for s in range(count)])
        for t in range(count)
    ]

    row_at = lax.broadcasted_iota(jnp.int32, (heads * group, 1), 0)
    request_at = lax.rem(row_at, group)
    lengths = jnp.zeros((heads * group, 1), jnp.int32)
    for r in range(group):
        lengths = jnp.where(request_at == r, lengths_ref[r], lengths)
    angles = lengths.astype(F32) * freq_ref[...]
    sine, cosine = sine_cosine(angles)
    lane = lax.broadcasted_iota(jnp.int32, (heads * group, head), 1)
    sine = jnp.where(lane < head // 2, -sine, sine)

    line = lax.broadcasted_iota(jnp.int32, (heads * group, lines), 1)
    slot = line // heads
    valid = (slot < lengths) & (line - slot * heads == row_at // group)
    bias[...] = jnp.where(valid, 0.0, -jnp.inf)

    blk_arrivals(0, lambda other: row_send, row_recv)
    wide_rows[...] = row_recv[...].astype(F32)
    normed = gather_lanes(wide_rows).astype(BF16)
    projected = []
    for k in range(3):
        loads[k].wait()
        projected.append(jnp.dot(normed, win[k], preferred_element_type=F32))
    finish(row_copies)

    scale = head ** (-0.5)

    def by_head(part):
        return jnp.concatenate([part[:, h * head : (h + 1) * head] for h in range(heads)], axis=0)

    query = rotate(by_head(projected[0]))
    key_new = rotate(by_head(projected[1]))
    value_new = by_head(projected[2]).astype(BF16).astype(F32)
    wide_query = query.astype(F32)
    own = scale * jnp.sum(wide_query * key_new.astype(F32), axis=-1, keepdims=True)
    scores = None
    for r in range(0, group, 2):
        key_loads[r].wait()
        key_loads[r + 1].wait()
        pair = jnp.concatenate(
            [jnp.where(request_at == r + i, wide_query, 0.0) for i in range(2)], axis=1
        ).astype(BF16)
        part = lax.dot_general(
            pair,
            jnp.concatenate([keys[r], keys[r + 1]], axis=1),
            (((1,), (1,)), ((), ())),
            preferred_element_type=F32,
        )
        scores = part if r == 0 else scores + part
    scores = scores * scale + bias[...]
    peak = jnp.maximum(jnp.max(scores, axis=-1, keepdims=True), own)
    shares = jnp.exp(scores - peak)
    own_share = jnp.exp(own - peak)
    denom = jnp.sum(shares, axis=-1, keepdims=True) + own_share
    shares = shares.astype(BF16)
    mixed = own_share * value_new
    for r in range(0, group, 2):
        value_loads[r].wait()
        value_loads[r + 1].wait()
        part = jnp.dot(
            shares,
            jnp.concatenate([values[r], values[r + 1]], axis=1),
            preferred_element_type=F32,
        )
        for i in range(2):
            mixed = mixed + jnp.where(
                request_at == r + i, part[:, i * head : (i + 1) * head], 0.0
            )
    mixed = (mixed / denom).astype(BF16)
    flat = jnp.concatenate(
        [mixed[h * group : (h + 1) * group] for h in range(heads)], axis=1
    )
    late[0].wait()
    scatter_lanes(wide_rows, jnp.dot(flat, wout[...], preferred_element_type=F32))
    attn_send[...] = wide_rows[...].astype(BF16)

    attn_copies = blk_exchange(1, lambda other: attn_send.at[other], attn_recv)
    attn_recv[blk] = attn_send[blk]
    blk_arrivals(1, lambda other: attn_send.at[other], attn_recv)
    attn_out = functools.reduce(lambda a, b: a + b, [attn_recv[j].astype(F32) for j in range(blk_count)])
    state = [mixed_state[t] + depth_ref[0, t] * attn_out for t in range(count)]
    row = functools.reduce(lambda a, b: a + b, [state[s] * width_ref[1, s] for s in range(count)])
    row = normalize(row)
    chunk = norm_send.shape[1]
    for c in range(req_count):
        norm_send[c] = row[c * chunk : (c + 1) * chunk]

    norm_copies = req_exchange(3, lambda other: norm_send.at[other], norm_recv)
    norm_recv[req] = norm_send[req]
    finish(attn_copies)
    req_arrivals(3, lambda other: norm_send.at[other], norm_recv)
    for c in range(req_count):
        joined[c * chunk : (c + 1) * chunk] = norm_recv[c]
    part_send[...] = joined[...].astype(BF16)
    part_copies = blk_exchange(2, lambda other: part_send, part_recv)
    part_recv[blk] = part_send[...]
    finish(norm_copies)
    mixed_state = [
        functools.reduce(lambda a, b: a + b, [state[s] * mix_ref[1, s, t] for s in range(count)])
        for t in range(count)
    ]
    late[1].wait()
    late[2].wait()
    blk_arrivals(2, lambda other: part_send, part_recv)
    wide_rows[...] = part_recv[...].astype(F32)
    columns = jnp.concatenate(
        [
            jnp.concatenate([wide_rows[:, c * chunk + k, :] for k in range(chunk)], axis=1)
            for c in range(req_count)
        ],
        axis=0,
    ).astype(BF16)
    half = wgate.shape[1] // 2

    def spread(part, landing):
        for c in range(req_count):
            rows = slice(c * group, (c + 1) * group)
            landing[c] = jnp.concatenate([part[rows, :half], part[rows, half:]], axis=0).astype(
                BF16
            )

    def total(landing):
        return functools.reduce(
            lambda a, b: a + b, [landing[c].astype(F32) for c in range(req_count)]
        )

    spread(jnp.dot(columns, wgate[...], preferred_element_type=F32), gate_send)
    gate_copies = req_exchange(0, lambda other: gate_send.at[other], gate_recv)
    spread(jnp.dot(columns, wup[...], preferred_element_type=F32), up_send)
    gate_copies += req_exchange(1, lambda other: up_send.at[other], up_recv)
    gate_recv[req] = gate_send[req]
    up_recv[req] = up_send[req]
    finish(part_copies)
    req_arrivals(0, lambda other: gate_send.at[other], gate_recv)
    gate = total(gate_recv)
    gate = gate / (1.0 + jnp.exp(-gate))
    req_arrivals(1, lambda other: up_send.at[other], up_recv)
    hid_send[...] = (gate * total(up_recv)).astype(BF16)

    hid_copies = req_exchange(2, lambda other: hid_send, hid_recv)
    hid_recv[req] = hid_send[...]
    finish(gate_copies)
    late[3].wait()
    req_arrivals(2, lambda other: hid_send, hid_recv)
    stacked = hid_recv[...].reshape(req_count * 2 * group, half)
    first = jnp.dot(stacked, wdown[:half], preferred_element_type=F32)
    second = jnp.dot(stacked, wdown[half:], preferred_element_type=F32)
    for c in range(req_count):
        low = 2 * group * c
        part = first[low : low + group] + second[low + group : low + 2 * group]
        for k in range(chunk):
            wide_rows[:, c * chunk + k, :] = part[:, k * LANES : (k + 1) * LANES]
    down_send[...] = wide_rows[...].astype(BF16)

    down_copies = blk_exchange(3, lambda other: down_send.at[other], down_recv)
    down_recv[blk] = down_send[blk]
    finish(hid_copies)
    blk_arrivals(3, lambda other: down_send.at[other], down_recv)
    joined[...] = functools.reduce(
        lambda a, b: a + b, [down_recv[j].astype(F32) for j in range(blk_count)]
    )
    for c in range(req_count):
        last_send[c] = joined[c * chunk : (c + 1) * chunk]
    last_copies = req_exchange(4, lambda other: last_send.at[other], last_recv)
    last_recv[req] = last_send[req]
    finish(down_copies)
    req_arrivals(4, lambda other: last_send.at[other], last_recv)
    for c in range(req_count):
        joined[c * chunk : (c + 1) * chunk] = last_recv[c]
    mlp_out = joined[...]
    for t in range(count):
        out_ref[0, t] = mixed_state[t] + depth_ref[1, t] * mlp_out
    finish(last_copies)


def on_device(
    hyper_state,
    lengths,
    key_cache,
    value_cache,
    attn_in_weight,
    attn_out_weight,
    w_gate,
    w_up,
    w_down,
    width_in,
    stream_mix,
    depth_out,
):
    req_count = lax.axis_size("req")
    blk_count = lax.axis_size("blk")
    _, count, width = hyper_state.shape
    group, heads, slots, head = key_cache.shape
    feature_part, hid_part = w_gate.shape
    parts = width // LANES
    chunk = feature_part // LANES
    freqs = np.exp(np.arange(head // 2) * (-2.0 * math.log(10000.0) / head))
    freqs = np.concatenate([freqs, freqs]).astype(np.float32)[None, :]
    vmem = pl.BlockSpec(memory_space=pltpu.VMEM)
    hbm = pl.BlockSpec(memory_space=pl.ANY)
    like = lambda x: pltpu.VMEM(x.shape, x.dtype)
    scalars = lambda x: pltpu.SMEM(x.shape, x.dtype)
    dma = pltpu.SemaphoreType.DMA
    lines = lambda x: jnp.transpose(x, (0, 2, 1, 3)).reshape(group, slots * heads, head)
    big = [lines(key_cache), lines(value_cache), attn_in_weight, attn_out_weight, w_gate, w_up, w_down]
    return pl.pallas_call(
        functools.partial(layer_kernel, req_count, blk_count),
        out_shape=jax.ShapeDtypeStruct((1, count, parts, LANES), F32),
        in_specs=[hbm] * (6 + len(big)),
        out_specs=vmem,
        scratch_shapes=[
            like(hyper_state),
            scalars(lengths),
            pltpu.VMEM(freqs.shape, F32),
            scalars(width_in),
            scalars(stream_mix),
            scalars(depth_out),
            pltpu.VMEM((heads * group, slots * heads), F32),
        ]
        + [like(x) for x in big]
        + [
            pltpu.VMEM((count, parts, LANES), F32),
            pltpu.VMEM((blk_count, parts, LANES), F32),
            pltpu.VMEM((parts, LANES), BF16),
            pltpu.VMEM((blk_count, parts, LANES), BF16),
            pltpu.VMEM((blk_count, parts, LANES), BF16),
            pltpu.VMEM((blk_count, parts, LANES), BF16),
            pltpu.VMEM((req_count, chunk, LANES), F32),
            pltpu.VMEM((req_count, chunk, LANES), F32),
            pltpu.VMEM((req_count, 2 * group, hid_part // 2), BF16),
            pltpu.VMEM((req_count, 2 * group, hid_part // 2), BF16),
            pltpu.VMEM((req_count, 2 * group, hid_part // 2), BF16),
            pltpu.VMEM((req_count, 2 * group, hid_part // 2), BF16),
            pltpu.VMEM((2 * group, hid_part // 2), BF16),
            pltpu.VMEM((req_count, 2 * group, hid_part // 2), BF16),
            pltpu.VMEM((blk_count, parts, LANES), BF16),
            pltpu.VMEM((blk_count, parts, LANES), BF16),
            pltpu.VMEM((parts, LANES), BF16),
            pltpu.VMEM((blk_count, parts, LANES), BF16),
            pltpu.VMEM((req_count, chunk, LANES), F32),
            pltpu.VMEM((req_count, chunk, LANES), F32),
            pltpu.VMEM((parts, LANES), F32),
            dma((6,)),
            dma((7,)),
            dma((group,)),
            dma((group,)),
            dma((4, blk_count - 1)),
            dma((4, blk_count - 1)),
            dma((5, req_count - 1)),
            dma((5, req_count - 1)),
        ],
        compiler_params=pltpu.CompilerParams(
            collective_id=0, has_side_effects=True, vmem_limit_bytes=56 * 2**20
        ),
        name="layer_step",
    )(hyper_state, lengths, jnp.asarray(freqs), width_in, stream_mix, depth_out, *big).reshape(hyper_state.shape)


def solution(mesh):
    placed = (
        P(("req", "blk"), None, None),
        P("req"),
        P("req", "blk", None, None),
        P("req", "blk", None, None),
        P(None, None, "blk"),
        P("blk", None),
        P("req", "blk"),
        P("req", "blk"),
        P("blk", "req"),
        P(),
        P(),
        P(),
    )
    return jax.shard_map(
        on_device,
        mesh=mesh,
        in_specs=placed,
        out_specs=P(("req", "blk"), None, None),
        check_vma=False,
    )
```

```python
import functools
import math

import jax
import jax.numpy as jnp
import numpy as np
from jax import lax
from jax.experimental import pallas as pl
from jax.experimental.pallas import tpu as pltpu
from jax.sharding import PartitionSpec as P

MESH = pl.DeviceIdType.MESH
LANES = 128
F32 = jnp.float32
BF16 = jnp.bfloat16


def split_two_pi():
    whole = 2.0 * math.pi
    one = float(np.round(whole * 2.0**8) / 2.0**8)
    two = float(np.round((whole - one) * 2.0**20) / 2.0**20)
    return one, two, whole - one - two


def sine_cosine(angles):
    one, two, three = split_two_pi()
    turns = jnp.floor(angles * (1.0 / (2.0 * math.pi)) + 0.5)
    rest = ((angles - turns * one) - turns * two) - turns * three
    return jnp.sin(rest), jnp.cos(rest)


def normalize(row):
    count = row.shape[0] * row.shape[1]
    center = row - jnp.sum(row, keepdims=True) * (1.0 / count)
    spread = jnp.sum(center * center, keepdims=True) * (1.0 / count)
    return center * lax.rsqrt(spread + 1e-05)


def gather_lanes(ref):
    return jnp.concatenate([ref[:, k, :] for k in range(ref.shape[1])], axis=1)


def scatter_lanes(ref, values):
    for k in range(ref.shape[1]):
        ref[:, k, :] = values[:, k * LANES : (k + 1) * LANES]


def wait_bytes(ref, sem):
    pltpu.make_async_copy(ref, ref, sem).wait()


def layer_kernel(
    req_count,
    blk_count,
    hyper_hbm,
    lengths_hbm,
    freq_hbm,
    width_hbm,
    mix_hbm,
    depth_hbm,
    keys_hbm,
    values_hbm,
    win_hbm,
    wout_hbm,
    wgate_hbm,
    wup_hbm,
    wdown_hbm,
    out_ref,
    hyper_ref,
    lengths_ref,
    freq_ref,
    width_ref,
    mix_ref,
    depth_ref,
    bias,
    keys,
    values,
    win,
    wout,
    wgate,
    wup,
    wdown,
    streams,
    wide_rows,
    row_send,
    row_recv,
    attn_send,
    attn_recv,
    norm_send,
    norm_recv,
    gate_send,
    gate_recv,
    up_send,
    up_recv,
    wide_down,
    down_send,
    down_recv,
    small_sem,
    load_sem,
    key_sem,
    value_sem,
    blk_send_sem,
    blk_recv_sem,
    req_send_sem,
    req_recv_sem,
    all_send_sem,
    all_recv_sem,
):
    req = lax.axis_index("req")
    blk = lax.axis_index("blk")
    everyone = req_count * blk_count
    me = req * blk_count + blk
    group, lines, head = keys.shape
    heads = win.shape[2] // head

    small = [
        pltpu.make_async_copy(src, dst, small_sem.at[i])
        for i, (src, dst) in enumerate(
            [
                (hyper_hbm, hyper_ref),
                (width_hbm, width_ref),
                (lengths_hbm, lengths_ref),
                (freq_hbm, freq_ref),
                (mix_hbm, mix_ref),
                (depth_hbm, depth_ref),
            ]
        )
    ]
    loads = [pltpu.make_async_copy(win_hbm.at[k], win.at[k], load_sem.at[k]) for k in range(3)]
    key_loads = [
        pltpu.make_async_copy(keys_hbm.at[r], keys.at[r], key_sem.at[r]) for r in range(group)
    ]
    value_loads = [
        pltpu.make_async_copy(values_hbm.at[r], values.at[r], value_sem.at[r])
        for r in range(group)
    ]
    sub = wdown.shape[1]

    def down_block(other):
        return wdown_hbm.at[pl.ds(pl.multiple_of(other * sub, sub), sub)]

    late = [
        pltpu.make_async_copy(src, dst, load_sem.at[3 + i])
        for i, (src, dst) in enumerate(
            [(wout_hbm, wout), (wgate_hbm, wgate), (wup_hbm, wup), (down_block(req), wdown.at[req])]
        )
    ]
    barrier = pltpu.get_barrier_semaphore()

    reqs = [req] + [lax.rem(req + d, req_count) for d in range(1, req_count)]
    blks = [blk] + [lax.rem(blk + d, blk_count) for d in range(1, blk_count)]
    peers = [
        (reqs[i], blks[j]) for i in range(req_count) for j in range(blk_count) if i + j > 0
    ]
    for copy in small + loads:
        copy.start()
    for peer in peers:
        pl.semaphore_signal(barrier, inc=1, device_id=peer, device_id_type=MESH)
    for copy in key_loads:
        copy.start()

    for copy in small:
        copy.wait()

    for k in range(streams.shape[1]):
        streams[:, k, :] = hyper_ref[0, :, k * LANES : (k + 1) * LANES]
    count = streams.shape[0]
    state = [streams[s] for s in range(count)]
    row = functools.reduce(lambda a, b: a + b, [state[s] * width_ref[0, s] for s in range(count)])
    row_send[...] = normalize(row).astype(BF16)

    pl.semaphore_wait(barrier, everyone - 1)

    def blk_copy(phase, d, source, landing, slot, other):
        return pltpu.make_async_remote_copy(
            src_ref=source,
            dst_ref=landing.at[slot],
            send_sem=blk_send_sem.at[phase, d - 1],
            recv_sem=blk_recv_sem.at[phase, d - 1],
            device_id=(req, other),
            device_id_type=MESH,
        )

    def blk_exchange(phase, source_of, landing):
        copies = [
            blk_copy(phase, d, source_of(blks[d]), landing, blk, blks[d])
            for d in range(1, blk_count)
        ]
        for copy in copies:
            copy.start()
        return copies

    def blk_arrivals(phase, source_of, landing):
        for d in range(1, blk_count):
            other = blks[blk_count - d]
            blk_copy(phase, d, source_of(other), landing, other, other).wait_recv()

    def req_copy(phase, d, source, landing, slot, other):
        return pltpu.make_async_remote_copy(
            src_ref=source,
            dst_ref=landing.at[slot],
            send_sem=req_send_sem.at[phase, d - 1],
            recv_sem=req_recv_sem.at[phase, d - 1],
            device_id=(other, blk),
            device_id_type=MESH,
        )

    def req_exchange(phase, source_of, landing):
        copies = [
            req_copy(phase, d, source_of(reqs[d]), landing, req, reqs[d])
            for d in range(1, req_count)
        ]
        for copy in copies:
            copy.start()
        return copies

    def req_arrivals(phase, source_of, landing):
        for d in range(1, req_count):
            other = reqs[req_count - d]
            req_copy(phase, d, source_of(other), landing, other, other).wait_recv()

    def all_exchange(phase, source_of, landing):
        for peer in peers:
            pltpu.make_async_remote_copy(
                src_ref=source_of(peer),
                dst_ref=landing.at[me],
                send_sem=all_send_sem.at[phase],
                recv_sem=all_recv_sem.at[phase],
                device_id=peer,
                device_id_type=MESH,
            ).start()

    def finish(copies):
        for copy in copies:
            copy.wait_send()

    row_copies = blk_exchange(0, lambda other: row_send, row_recv)
    for copy in value_loads + late:
        copy.start()
    weight_copies = req_exchange(2, down_block, wdown)
    row_recv[blk] = row_send[...]

    def rotate(part):
        return (part * cosine + pltpu.roll(part, head // 2, 1) * sine).astype(BF16)

    mixed_state = [
        functools.reduce(lambda a, b: a + b, [state[s] * mix_ref[0, s, t] for s in range(count)])
        for t in range(count)
    ]

    row_at = lax.broadcasted_iota(jnp.int32, (heads * group, 1), 0)
    request_at = lax.rem(row_at, group)
    lengths = jnp.zeros((heads * group, 1), jnp.int32)
    for r in range(group):
        lengths = jnp.where(request_at == r, lengths_ref[r], lengths)
    angles = lengths.astype(F32) * freq_ref[...]
    sine, cosine = sine_cosine(angles)
    lane = lax.broadcasted_iota(jnp.int32, (heads * group, head), 1)
    sine = jnp.where(lane < head // 2, -sine, sine)

    line = lax.broadcasted_iota(jnp.int32, (heads * group, lines), 1)
    slot = line // heads
    valid = (slot < lengths) & (line - slot * heads == row_at // group)
    bias[...] = jnp.where(valid, 0.0, -jnp.inf)

    blk_arrivals(0, lambda other: row_send, row_recv)
    wide_rows[...] = row_recv[...].astype(F32)
    normed = gather_lanes(wide_rows).astype(BF16)
    projected = []
    for k in range(3):
        loads[k].wait()
        projected.append(jnp.dot(normed, win[k], preferred_element_type=F32))
    finish(row_copies)

    scale = head ** (-0.5)

    def by_head(part):
        return jnp.concatenate([part[:, h * head : (h + 1) * head] for h in range(heads)], axis=0)

    query = rotate(by_head(projected[0]))
    key_new = rotate(by_head(projected[1]))
    value_new = by_head(projected[2]).astype(BF16).astype(F32)
    wide_query = query.astype(F32)
    own = scale * jnp.sum(wide_query * key_new.astype(F32), axis=-1, keepdims=True)
    scores = None
    for r in range(0, group, 2):
        key_loads[r].wait()
        key_loads[r + 1].wait()
        pair = jnp.concatenate(
            [jnp.where(request_at == r + i, wide_query, 0.0) for i in range(2)], axis=1
        ).astype(BF16)
        part = lax.dot_general(
            pair,
            jnp.concatenate([keys[r], keys[r + 1]], axis=1),
            (((1,), (1,)), ((), ())),
            preferred_element_type=F32,
        )
        scores = part if r == 0 else scores + part
    scores = scores * scale + bias[...]
    peak = jnp.maximum(jnp.max(scores, axis=-1, keepdims=True), own)
    shares = jnp.exp(scores - peak)
    own_share = jnp.exp(own - peak)
    denom = jnp.sum(shares, axis=-1, keepdims=True) + own_share
    shares = shares.astype(BF16)
    mixed = own_share * value_new
    for r in range(0, group, 2):
        value_loads[r].wait()
        value_loads[r + 1].wait()
        part = jnp.dot(
            shares,
            jnp.concatenate([values[r], values[r + 1]], axis=1),
            preferred_element_type=F32,
        )
        for i in range(2):
            mixed = mixed + jnp.where(
                request_at == r + i, part[:, i * head : (i + 1) * head], 0.0
            )
    mixed = (mixed / denom).astype(BF16)
    flat = jnp.concatenate(
        [mixed[h * group : (h + 1) * group] for h in range(heads)], axis=1
    )
    late[0].wait()
    scatter_lanes(wide_rows, jnp.dot(flat, wout[...], preferred_element_type=F32))
    attn_send[...] = wide_rows[...].astype(BF16)

    attn_copies = blk_exchange(1, lambda other: attn_send.at[other], attn_recv)
    attn_recv[blk] = attn_send[blk]
    blk_arrivals(1, lambda other: attn_send.at[other], attn_recv)
    attn_out = functools.reduce(lambda a, b: a + b, [attn_recv[j].astype(F32) for j in range(blk_count)])
    state = [mixed_state[t] + depth_ref[0, t] * attn_out for t in range(count)]
    row = functools.reduce(lambda a, b: a + b, [state[s] * width_ref[1, s] for s in range(count)])
    row = normalize(row)
    chunk = norm_send.shape[1]
    for c in range(req_count):
        norm_send[c] = row[c * chunk : (c + 1) * chunk]

    all_exchange(0, lambda peer: norm_send.at[peer[0]], norm_recv)
    norm_recv[me] = norm_send[req]
    finish(attn_copies)
    mixed_state = [
        functools.reduce(lambda a, b: a + b, [state[s] * mix_ref[1, s, t] for s in range(count)])
        for t in range(count)
    ]
    others = pl.ds(0, everyone - 1)
    late[1].wait()
    late[2].wait()
    wait_bytes(norm_recv.at[others], all_recv_sem.at[0])
    columns = gather_lanes(norm_recv).astype(BF16)

    def spread(part, landing):
        for c in range(req_count):
            landing[c] = part[:, c * sub : (c + 1) * sub].astype(BF16)

    def total(landing):
        return functools.reduce(
            lambda a, b: a + b, [landing[c].astype(F32) for c in range(req_count)]
        )

    spread(jnp.dot(columns, wgate[...], preferred_element_type=F32), gate_send)
    gate_copies = req_exchange(0, lambda other: gate_send.at[other], gate_recv)
    spread(jnp.dot(columns, wup[...], preferred_element_type=F32), up_send)
    gate_copies += req_exchange(1, lambda other: up_send.at[other], up_recv)
    gate_recv[req] = gate_send[req]
    up_recv[req] = up_send[req]
    wait_bytes(norm_recv.at[others], all_send_sem.at[0])
    req_arrivals(0, lambda other: gate_send.at[other], gate_recv)
    gate = total(gate_recv)
    gate = gate / (1.0 + jnp.exp(-gate))
    req_arrivals(1, lambda other: up_send.at[other], up_recv)
    hidden = (gate * total(up_recv)).astype(BF16)

    finish(weight_copies)
    late[3].wait()
    req_arrivals(2, down_block, wdown)
    for c in range(req_count):
        part = jnp.dot(hidden, wdown[c], preferred_element_type=F32)
        for k in range(chunk):
            wide_down[:, c * chunk + k, :] = part[:, k * LANES : (k + 1) * LANES]
    down_send[...] = wide_down[...].astype(BF16)
    all_exchange(1, lambda peer: down_send.at[peer[0] * blk_count + peer[1]], down_recv)
    down_recv[me] = down_send[me]
    finish(gate_copies)
    wait_bytes(down_recv.at[others], all_recv_sem.at[1])
    mlp_out = functools.reduce(
        lambda a, b: a + b, [down_recv[j].astype(F32) for j in range(everyone)]
    )
    for t in range(count):
        out_ref[0, t] = mixed_state[t] + depth_ref[1, t] * mlp_out
    wait_bytes(down_recv.at[others], all_send_sem.at[1])


def on_device(
    hyper_state,
    lengths,
    key_cache,
    value_cache,
    attn_in_weight,
    attn_out_weight,
    w_gate,
    w_up,
    w_down,
    width_in,
    stream_mix,
    depth_out,
):
    req_count = lax.axis_size("req")
    blk_count = lax.axis_size("blk")
    everyone = req_count * blk_count
    _, count, width = hyper_state.shape
    group, heads, slots, head = key_cache.shape
    feature_part, hid_part = w_gate.shape
    parts = width // LANES
    sub = hid_part // req_count
    chunk = feature_part // LANES
    freqs = np.exp(np.arange(head // 2) * (-2.0 * math.log(10000.0) / head))
    freqs = np.concatenate([freqs, freqs]).astype(np.float32)[None, :]
    vmem = pl.BlockSpec(memory_space=pltpu.VMEM)
    hbm = pl.BlockSpec(memory_space=pl.ANY)
    like = lambda x: pltpu.VMEM(x.shape, x.dtype)
    scalars = lambda x: pltpu.SMEM(x.shape, x.dtype)
    dma = pltpu.SemaphoreType.DMA
    lines = lambda x: jnp.transpose(x, (0, 2, 1, 3)).reshape(group, slots * heads, head)
    big = [lines(key_cache), lines(value_cache), attn_in_weight, attn_out_weight, w_gate, w_up, w_down]
    return pl.pallas_call(
        functools.partial(layer_kernel, req_count, blk_count),
        out_shape=jax.ShapeDtypeStruct((1, count, parts, LANES), F32),
        in_specs=[hbm] * (6 + len(big)),
        out_specs=vmem,
        scratch_shapes=[
            like(hyper_state),
            scalars(lengths),
            pltpu.VMEM(freqs.shape, F32),
            scalars(width_in),
            scalars(stream_mix),
            scalars(depth_out),
            pltpu.VMEM((heads * group, slots * heads), F32),
        ]
        + [like(x) for x in big[:-1]]
        + [pltpu.VMEM((req_count, sub, w_down.shape[1]), BF16)]
        + [
            pltpu.VMEM((count, parts, LANES), F32),
            pltpu.VMEM((blk_count, parts, LANES), F32),
            pltpu.VMEM((parts, LANES), BF16),
            pltpu.VMEM((blk_count, parts, LANES), BF16),
            pltpu.VMEM((blk_count, parts, LANES), BF16),
            pltpu.VMEM((blk_count, parts, LANES), BF16),
            pltpu.VMEM((req_count, chunk, LANES), F32),
            pltpu.VMEM((everyone, chunk, LANES), F32),
            pltpu.VMEM((req_count, everyone, sub), BF16),
            pltpu.VMEM((req_count, everyone, sub), BF16),
            pltpu.VMEM((req_count, everyone, sub), BF16),
            pltpu.VMEM((req_count, everyone, sub), BF16),
            pltpu.VMEM((everyone, parts, LANES), F32),
            pltpu.VMEM((everyone, parts, LANES), BF16),
            pltpu.VMEM((everyone, parts, LANES), BF16),
            dma((6,)),
            dma((7,)),
            dma((group,)),
            dma((group,)),
            dma((2, blk_count - 1)),
            dma((2, blk_count - 1)),
            dma((3, req_count - 1)),
            dma((3, req_count - 1)),
            dma((2,)),
            dma((2,)),
        ],
        compiler_params=pltpu.CompilerParams(
            collective_id=0, has_side_effects=True, vmem_limit_bytes=56 * 2**20
        ),
        name="layer_step",
    )(hyper_state, lengths, jnp.asarray(freqs), width_in, stream_mix, depth_out, *big).reshape(hyper_state.shape)


def solution(mesh):
    placed = (
        P(("req", "blk"), None, None),
        P("req"),
        P("req", "blk", None, None),
        P("req", "blk", None, None),
        P(None, None, "blk"),
        P("blk", None),
        P("req", "blk"),
        P("req", "blk"),
        P("blk", "req"),
        P(),
        P(),
        P(),
    )
    return jax.shard_map(
        on_device,
        mesh=mesh,
        in_specs=placed,
        out_specs=P(("req", "blk"), None, None),
        check_vma=False,
    )
```

```python
import functools
import math

import jax
import jax.numpy as jnp
import numpy as np
from jax import lax
from jax.experimental import pallas as pl
from jax.experimental.pallas import tpu as pltpu
from jax.sharding import PartitionSpec as P

MESH = pl.DeviceIdType.MESH
LANES = 128
F32 = jnp.float32
BF16 = jnp.bfloat16


def split_two_pi():
    whole = 2.0 * math.pi
    one = float(np.round(whole * 2.0**8) / 2.0**8)
    two = float(np.round((whole - one) * 2.0**20) / 2.0**20)
    return one, two, whole - one - two


def sine_cosine(angles):
    one, two, three = split_two_pi()
    turns = jnp.floor(angles * (1.0 / (2.0 * math.pi)) + 0.5)
    rest = ((angles - turns * one) - turns * two) - turns * three
    return jnp.sin(rest), jnp.cos(rest)


def normalize(row):
    count = row.shape[0] * row.shape[1]
    center = row - jnp.sum(row, keepdims=True) * (1.0 / count)
    spread = jnp.sum(center * center, keepdims=True) * (1.0 / count)
    return center * lax.rsqrt(spread + 1e-05)


def gather_lanes(ref):
    return jnp.concatenate([ref[:, k, :] for k in range(ref.shape[1])], axis=1)


def scatter_lanes(ref, values):
    for k in range(ref.shape[1]):
        ref[:, k, :] = values[:, k * LANES : (k + 1) * LANES]


def wait_bytes(ref, sem):
    pltpu.make_async_copy(ref, ref, sem).wait()


def layer_kernel(
    req_count,
    blk_count,
    hyper_hbm,
    lengths_hbm,
    freq_hbm,
    width_hbm,
    mix_hbm,
    depth_hbm,
    keys_hbm,
    values_hbm,
    win_hbm,
    wout_hbm,
    wgate_hbm,
    wup_hbm,
    wdown_hbm,
    out_ref,
    hyper_ref,
    lengths_ref,
    freq_ref,
    width_ref,
    mix_ref,
    depth_ref,
    bias,
    keys_turned,
    keys,
    values,
    win,
    wout,
    wgate,
    wup,
    wdown,
    streams,
    wide_rows,
    row_send,
    row_recv,
    attn_send,
    attn_recv,
    norm_send,
    norm_recv,
    gate_send,
    gate_recv,
    up_send,
    up_recv,
    wide_down,
    down_send,
    down_recv,
    small_sem,
    load_sem,
    key_sem,
    value_sem,
    blk_send_sem,
    blk_recv_sem,
    req_send_sem,
    req_recv_sem,
    all_send_sem,
    all_recv_sem,
):
    req = lax.axis_index("req")
    blk = lax.axis_index("blk")
    everyone = req_count * blk_count
    me = req * blk_count + blk
    group, lines, head = keys.shape
    heads = win.shape[2] // head

    small = [
        pltpu.make_async_copy(src, dst, small_sem.at[i])
        for i, (src, dst) in enumerate(
            [
                (hyper_hbm, hyper_ref),
                (width_hbm, width_ref),
                (lengths_hbm, lengths_ref),
                (freq_hbm, freq_ref),
                (mix_hbm, mix_ref),
                (depth_hbm, depth_ref),
            ]
        )
    ]
    loads = [pltpu.make_async_copy(win_hbm.at[k], win.at[k], load_sem.at[k]) for k in range(3)]
    key_loads = [
        pltpu.make_async_copy(keys_hbm.at[r], keys.at[r], key_sem.at[r]) for r in range(group)
    ]
    value_loads = [
        pltpu.make_async_copy(values_hbm.at[r], values.at[r], value_sem.at[r])
        for r in range(group)
    ]
    sub = wdown.shape[1]

    def down_block(other):
        return wdown_hbm.at[pl.ds(pl.multiple_of(other * sub, sub), sub)]

    late = [
        pltpu.make_async_copy(src, dst, load_sem.at[3 + i])
        for i, (src, dst) in enumerate(
            [(wout_hbm, wout), (wgate_hbm, wgate), (wup_hbm, wup), (down_block(req), wdown.at[req])]
        )
    ]
    barrier = pltpu.get_barrier_semaphore()

    reqs = [req] + [lax.rem(req + d, req_count) for d in range(1, req_count)]
    blks = [blk] + [lax.rem(blk + d, blk_count) for d in range(1, blk_count)]
    peers = [
        (reqs[i], blks[j]) for i in range(req_count) for j in range(blk_count) if i + j > 0
    ]
    for copy in small + loads:
        copy.start()
    for peer in peers:
        pl.semaphore_signal(barrier, inc=1, device_id=peer, device_id_type=MESH)
    for copy in key_loads:
        copy.start()

    for copy in small:
        copy.wait()

    for k in range(streams.shape[1]):
        streams[:, k, :] = hyper_ref[0, :, k * LANES : (k + 1) * LANES]
    count = streams.shape[0]
    state = [streams[s] for s in range(count)]
    row = functools.reduce(lambda a, b: a + b, [state[s] * width_ref[0, s] for s in range(count)])
    row_send[...] = normalize(row).astype(BF16)

    pl.semaphore_wait(barrier, everyone - 1)

    def blk_copy(phase, d, source, landing, slot, other):
        return pltpu.make_async_remote_copy(
            src_ref=source,
            dst_ref=landing.at[slot],
            send_sem=blk_send_sem.at[phase, d - 1],
            recv_sem=blk_recv_sem.at[phase, d - 1],
            device_id=(req, other),
            device_id_type=MESH,
        )

    def blk_exchange(phase, source_of, landing):
        copies = [
            blk_copy(phase, d, source_of(blks[d]), landing, blk, blks[d])
            for d in range(1, blk_count)
        ]
        for copy in copies:
            copy.start()
        return copies

    def blk_arrivals(phase, source_of, landing):
        for d in range(1, blk_count):
            other = blks[blk_count - d]
            blk_copy(phase, d, source_of(other), landing, other, other).wait_recv()

    def req_copy(phase, d, source, landing, slot, other):
        return pltpu.make_async_remote_copy(
            src_ref=source,
            dst_ref=landing.at[slot],
            send_sem=req_send_sem.at[phase, d - 1],
            recv_sem=req_recv_sem.at[phase, d - 1],
            device_id=(other, blk),
            device_id_type=MESH,
        )

    def req_exchange(phase, source_of, landing):
        copies = [
            req_copy(phase, d, source_of(reqs[d]), landing, req, reqs[d])
            for d in range(1, req_count)
        ]
        for copy in copies:
            copy.start()
        return copies

    def req_arrivals(phase, source_of, landing):
        for d in range(1, req_count):
            other = reqs[req_count - d]
            req_copy(phase, d, source_of(other), landing, other, other).wait_recv()

    def all_exchange(phase, source_of, landing):
        for peer in peers:
            pltpu.make_async_remote_copy(
                src_ref=source_of(peer),
                dst_ref=landing.at[me],
                send_sem=all_send_sem.at[phase],
                recv_sem=all_recv_sem.at[phase],
                device_id=peer,
                device_id_type=MESH,
            ).start()

    def finish(copies):
        for copy in copies:
            copy.wait_send()

    row_copies = blk_exchange(0, lambda other: row_send, row_recv)
    for copy in value_loads + late:
        copy.start()
    weight_copies = req_exchange(2, down_block, wdown)
    row_recv[blk] = row_send[...]

    def rotate(part):
        return (part * cosine + pltpu.roll(part, head // 2, 1) * sine).astype(BF16)

    mixed_state = [
        functools.reduce(lambda a, b: a + b, [state[s] * mix_ref[0, s, t] for s in range(count)])
        for t in range(count)
    ]

    row_at = lax.broadcasted_iota(jnp.int32, (heads * group, 1), 0)
    request_at = lax.rem(row_at, group)
    lengths = jnp.zeros((heads * group, 1), jnp.int32)
    for r in range(group):
        lengths = jnp.where(request_at == r, lengths_ref[r], lengths)
    angles = lengths.astype(F32) * freq_ref[...]
    sine, cosine = sine_cosine(angles)
    lane = lax.broadcasted_iota(jnp.int32, (heads * group, head), 1)
    sine = jnp.where(lane < head // 2, -sine, sine)

    line = lax.broadcasted_iota(jnp.int32, (heads * group, lines), 1)
    slot = line // heads
    valid = (slot < lengths) & (line - slot * heads == row_at // group)
    bias[...] = jnp.where(valid, 0.0, -jnp.inf)

    for r in range(group):
        key_loads[r].wait()
        keys_turned[r] = jnp.transpose(keys[r])

    blk_arrivals(0, lambda other: row_send, row_recv)
    wide_rows[...] = row_recv[...].astype(F32)
    normed = gather_lanes(wide_rows).astype(BF16)
    projected = []
    for k in range(3):
        loads[k].wait()
        projected.append(jnp.dot(normed, win[k], preferred_element_type=F32))
    finish(row_copies)

    scale = head ** (-0.5)

    def by_head(part):
        return jnp.concatenate([part[:, h * head : (h + 1) * head] for h in range(heads)], axis=0)

    query = rotate(by_head(projected[0]))
    key_new = rotate(by_head(projected[1]))
    value_new = by_head(projected[2]).astype(BF16).astype(F32)
    wide_query = query.astype(F32)
    own = scale * jnp.sum(wide_query * key_new.astype(F32), axis=-1, keepdims=True)
    scores = None
    for r in range(0, group, 2):
        pair = jnp.concatenate(
            [jnp.where(request_at == r + i, wide_query, 0.0) for i in range(2)], axis=1
        ).astype(BF16)
        part = jnp.dot(
            pair,
            jnp.concatenate([keys_turned[r], keys_turned[r + 1]], axis=0),
            preferred_element_type=F32,
        )
        scores = part if r == 0 else scores + part
    scores = scores * scale + bias[...]
    peak = jnp.maximum(jnp.max(scores, axis=-1, keepdims=True), own)
    shares = jnp.exp(scores - peak)
    own_share = jnp.exp(own - peak)
    denom = jnp.sum(shares, axis=-1, keepdims=True) + own_share
    shares = shares.astype(BF16)
    mixed = own_share * value_new
    for r in range(0, group, 2):
        value_loads[r].wait()
        value_loads[r + 1].wait()
        part = jnp.dot(
            shares,
            jnp.concatenate([values[r], values[r + 1]], axis=1),
            preferred_element_type=F32,
        )
        for i in range(2):
            mixed = mixed + jnp.where(
                request_at == r + i, part[:, i * head : (i + 1) * head], 0.0
            )
    mixed = (mixed / denom).astype(BF16)
    flat = jnp.concatenate(
        [mixed[h * group : (h + 1) * group] for h in range(heads)], axis=1
    )
    late[0].wait()
    scatter_lanes(wide_rows, jnp.dot(flat, wout[...], preferred_element_type=F32))
    attn_send[...] = wide_rows[...].astype(BF16)

    attn_copies = blk_exchange(1, lambda other: attn_send.at[other], attn_recv)
    attn_recv[blk] = attn_send[blk]
    blk_arrivals(1, lambda other: attn_send.at[other], attn_recv)
    attn_out = functools.reduce(lambda a, b: a + b, [attn_recv[j].astype(F32) for j in range(blk_count)])
    state = [mixed_state[t] + depth_ref[0, t] * attn_out for t in range(count)]
    row = functools.reduce(lambda a, b: a + b, [state[s] * width_ref[1, s] for s in range(count)])
    row = normalize(row)
    chunk = norm_send.shape[1]
    for c in range(req_count):
        norm_send[c] = row[c * chunk : (c + 1) * chunk]

    all_exchange(0, lambda peer: norm_send.at[peer[0]], norm_recv)
    norm_recv[me] = norm_send[req]
    finish(attn_copies)
    mixed_state = [
        functools.reduce(lambda a, b: a + b, [state[s] * mix_ref[1, s, t] for s in range(count)])
        for t in range(count)
    ]
    others = pl.ds(0, everyone - 1)
    late[1].wait()
    late[2].wait()
    wait_bytes(norm_recv.at[others], all_recv_sem.at[0])
    columns = gather_lanes(norm_recv).astype(BF16)

    def spread(part, landing):
        for c in range(req_count):
            landing[c] = part[:, c * sub : (c + 1) * sub].astype(BF16)

    def total(landing):
        return functools.reduce(
            lambda a, b: a + b, [landing[c].astype(F32) for c in range(req_count)]
        )

    spread(jnp.dot(columns, wgate[...], preferred_element_type=F32), gate_send)
    gate_copies = req_exchange(0, lambda other: gate_send.at[other], gate_recv)
    spread(jnp.dot(columns, wup[...], preferred_element_type=F32), up_send)
    gate_copies += req_exchange(1, lambda other: up_send.at[other], up_recv)
    gate_recv[req] = gate_send[req]
    up_recv[req] = up_send[req]
    wait_bytes(norm_recv.at[others], all_send_sem.at[0])
    req_arrivals(0, lambda other: gate_send.at[other], gate_recv)
    gate = total(gate_recv)
    gate = gate / (1.0 + jnp.exp(-gate))
    req_arrivals(1, lambda other: up_send.at[other], up_recv)
    hidden = (gate * total(up_recv)).astype(BF16)

    finish(weight_copies)
    late[3].wait()
    req_arrivals(2, down_block, wdown)
    for c in range(req_count):
        part = jnp.dot(hidden, wdown[c], preferred_element_type=F32)
        for k in range(chunk):
            wide_down[:, c * chunk + k, :] = part[:, k * LANES : (k + 1) * LANES]
    down_send[...] = wide_down[...].astype(BF16)
    all_exchange(1, lambda peer: down_send.at[peer[0] * blk_count + peer[1]], down_recv)
    down_recv[me] = down_send[me]
    finish(gate_copies)
    wait_bytes(down_recv.at[others], all_recv_sem.at[1])
    mlp_out = functools.reduce(
        lambda a, b: a + b, [down_recv[j].astype(F32) for j in range(everyone)]
    )
    for t in range(count):
        out_ref[0, t] = mixed_state[t] + depth_ref[1, t] * mlp_out
    wait_bytes(down_recv.at[others], all_send_sem.at[1])


def on_device(
    hyper_state,
    lengths,
    key_cache,
    value_cache,
    attn_in_weight,
    attn_out_weight,
    w_gate,
    w_up,
    w_down,
    width_in,
    stream_mix,
    depth_out,
):
    req_count = lax.axis_size("req")
    blk_count = lax.axis_size("blk")
    everyone = req_count * blk_count
    _, count, width = hyper_state.shape
    group, heads, slots, head = key_cache.shape
    feature_part, hid_part = w_gate.shape
    parts = width // LANES
    sub = hid_part // req_count
    chunk = feature_part // LANES
    freqs = np.exp(np.arange(head // 2) * (-2.0 * math.log(10000.0) / head))
    freqs = np.concatenate([freqs, freqs]).astype(np.float32)[None, :]
    vmem = pl.BlockSpec(memory_space=pltpu.VMEM)
    hbm = pl.BlockSpec(memory_space=pl.ANY)
    like = lambda x: pltpu.VMEM(x.shape, x.dtype)
    scalars = lambda x: pltpu.SMEM(x.shape, x.dtype)
    dma = pltpu.SemaphoreType.DMA
    lines = lambda x: jnp.transpose(x, (0, 2, 1, 3)).reshape(group, slots * heads, head)
    big = [lines(key_cache), lines(value_cache), attn_in_weight, attn_out_weight, w_gate, w_up, w_down]
    return pl.pallas_call(
        functools.partial(layer_kernel, req_count, blk_count),
        out_shape=jax.ShapeDtypeStruct((1, count, parts, LANES), F32),
        in_specs=[hbm] * (6 + len(big)),
        out_specs=vmem,
        scratch_shapes=[
            like(hyper_state),
            scalars(lengths),
            pltpu.VMEM(freqs.shape, F32),
            scalars(width_in),
            scalars(stream_mix),
            scalars(depth_out),
            pltpu.VMEM((heads * group, slots * heads), F32),
            pltpu.VMEM((group, head, slots * heads), BF16),
        ]
        + [like(x) for x in big[:-1]]
        + [pltpu.VMEM((req_count, sub, w_down.shape[1]), BF16)]
        + [
            pltpu.VMEM((count, parts, LANES), F32),
            pltpu.VMEM((blk_count, parts, LANES), F32),
            pltpu.VMEM((parts, LANES), BF16),
            pltpu.VMEM((blk_count, parts, LANES), BF16),
            pltpu.VMEM((blk_count, parts, LANES), BF16),
            pltpu.VMEM((blk_count, parts, LANES), BF16),
            pltpu.VMEM((req_count, chunk, LANES), F32),
            pltpu.VMEM((everyone, chunk, LANES), F32),
            pltpu.VMEM((req_count, everyone, sub), BF16),
            pltpu.VMEM((req_count, everyone, sub), BF16),
            pltpu.VMEM((req_count, everyone, sub), BF16),
            pltpu.VMEM((req_count, everyone, sub), BF16),
            pltpu.VMEM((everyone, parts, LANES), F32),
            pltpu.VMEM((everyone, parts, LANES), BF16),
            pltpu.VMEM((everyone, parts, LANES), BF16),
            dma((6,)),
            dma((7,)),
            dma((group,)),
            dma((group,)),
            dma((2, blk_count - 1)),
            dma((2, blk_count - 1)),
            dma((3, req_count - 1)),
            dma((3, req_count - 1)),
            dma((2,)),
            dma((2,)),
        ],
        compiler_params=pltpu.CompilerParams(
            collective_id=0, has_side_effects=True, vmem_limit_bytes=56 * 2**20
        ),
        name="layer_step",
    )(hyper_state, lengths, jnp.asarray(freqs), width_in, stream_mix, depth_out, *big).reshape(hyper_state.shape)


def solution(mesh):
    placed = (
        P(("req", "blk"), None, None),
        P("req"),
        P("req", "blk", None, None),
        P("req", "blk", None, None),
        P(None, None, "blk"),
        P("blk", None),
        P("req", "blk"),
        P("req", "blk"),
        P("blk", "req"),
        P(),
        P(),
        P(),
    )
    return jax.shard_map(
        on_device,
        mesh=mesh,
        in_specs=placed,
        out_specs=P(("req", "blk"), None, None),
        check_vma=False,
    )
```

```python
import functools
import math

import jax
import jax.numpy as jnp
import numpy as np
from jax import lax
from jax.experimental import pallas as pl
from jax.experimental.pallas import tpu as pltpu
from jax.sharding import PartitionSpec as P

MESH = pl.DeviceIdType.MESH
LANES = 128
F32 = jnp.float32
BF16 = jnp.bfloat16


def split_two_pi():
    whole = 2.0 * math.pi
    one = float(np.round(whole * 2.0**8) / 2.0**8)
    two = float(np.round((whole - one) * 2.0**20) / 2.0**20)
    return one, two, whole - one - two


def sine_cosine(angles):
    one, two, three = split_two_pi()
    turns = jnp.floor(angles * (1.0 / (2.0 * math.pi)) + 0.5)
    rest = ((angles - turns * one) - turns * two) - turns * three
    return jnp.sin(rest), jnp.cos(rest)


def normalize(row):
    count = row.shape[0] * row.shape[1]
    center = row - jnp.sum(row, keepdims=True) * (1.0 / count)
    spread = jnp.sum(center * center, keepdims=True) * (1.0 / count)
    return center * lax.rsqrt(spread + 1e-05)


def gather_lanes(ref):
    return jnp.concatenate([ref[:, k, :] for k in range(ref.shape[1])], axis=1)


def scatter_lanes(ref, values):
    for k in range(ref.shape[1]):
        ref[:, k, :] = values[:, k * LANES : (k + 1) * LANES]


def wait_bytes(ref, sem):
    pltpu.make_async_copy(ref, ref, sem).wait()


def layer_kernel(
    req_count,
    blk_count,
    hyper_hbm,
    lengths_hbm,
    freq_hbm,
    width_hbm,
    mix_hbm,
    depth_hbm,
    keys_hbm,
    values_hbm,
    win_hbm,
    wout_hbm,
    wgate_hbm,
    wup_hbm,
    wdown_hbm,
    out_ref,
    hyper_ref,
    lengths_ref,
    freq_ref,
    width_ref,
    mix_ref,
    depth_ref,
    bias,
    keys_turned,
    keys,
    values,
    win,
    wout,
    wgate,
    wup,
    wdown,
    streams,
    wide_rows,
    row_send,
    row_recv,
    attn_send,
    attn_recv,
    norm_send,
    norm_recv,
    gate_send,
    gate_recv,
    up_send,
    up_recv,
    wide_down,
    down_send,
    down_recv,
    small_sem,
    load_sem,
    key_sem,
    value_sem,
    blk_send_sem,
    blk_recv_sem,
    req_send_sem,
    req_recv_sem,
    all_send_sem,
    all_recv_sem,
):
    req = lax.axis_index("req")
    blk = lax.axis_index("blk")
    everyone = req_count * blk_count
    me = req * blk_count + blk
    group, lines, head = keys.shape
    heads = win.shape[2] // head

    small = [
        pltpu.make_async_copy(src, dst, small_sem.at[i])
        for i, (src, dst) in enumerate(
            [
                (hyper_hbm, hyper_ref),
                (width_hbm, width_ref),
                (lengths_hbm, lengths_ref),
                (freq_hbm, freq_ref),
                (mix_hbm, mix_ref),
                (depth_hbm, depth_ref),
            ]
        )
    ]
    loads = [pltpu.make_async_copy(win_hbm.at[k], win.at[k], load_sem.at[k]) for k in range(3)]
    key_loads = [
        pltpu.make_async_copy(keys_hbm.at[r], keys.at[r], key_sem.at[r]) for r in range(group)
    ]
    value_loads = [
        pltpu.make_async_copy(
            values_hbm.at[r], values.at[:, pl.ds(r * head, head)], value_sem.at[r]
        )
        for r in range(group)
    ]
    sub = wdown.shape[1]

    def down_block(other):
        return wdown_hbm.at[pl.ds(pl.multiple_of(other * sub, sub), sub)]

    late = [
        pltpu.make_async_copy(src, dst, load_sem.at[3 + i])
        for i, (src, dst) in enumerate(
            [(wout_hbm, wout), (wgate_hbm, wgate), (wup_hbm, wup), (down_block(req), wdown.at[req])]
        )
    ]
    barrier = pltpu.get_barrier_semaphore()

    reqs = [req] + [lax.rem(req + d, req_count) for d in range(1, req_count)]
    blks = [blk] + [lax.rem(blk + d, blk_count) for d in range(1, blk_count)]
    peers = [
        (reqs[i], blks[j]) for i in range(req_count) for j in range(blk_count) if i + j > 0
    ]
    for copy in small + loads:
        copy.start()
    for peer in peers:
        pl.semaphore_signal(barrier, inc=1, device_id=peer, device_id_type=MESH)
    for copy in key_loads:
        copy.start()

    for copy in small:
        copy.wait()

    for k in range(streams.shape[1]):
        streams[:, k, :] = hyper_ref[0, :, k * LANES : (k + 1) * LANES]
    count = streams.shape[0]
    state = [streams[s] for s in range(count)]
    row = functools.reduce(lambda a, b: a + b, [state[s] * width_ref[0, s] for s in range(count)])
    row_send[...] = normalize(row).astype(BF16)

    pl.semaphore_wait(barrier, everyone - 1)

    def blk_copy(phase, d, source, landing, slot, other):
        return pltpu.make_async_remote_copy(
            src_ref=source,
            dst_ref=landing.at[slot],
            send_sem=blk_send_sem.at[phase, d - 1],
            recv_sem=blk_recv_sem.at[phase, d - 1],
            device_id=(req, other),
            device_id_type=MESH,
        )

    def blk_exchange(phase, source_of, landing):
        copies = [
            blk_copy(phase, d, source_of(blks[d]), landing, blk, blks[d])
            for d in range(1, blk_count)
        ]
        for copy in copies:
            copy.start()
        return copies

    def blk_arrivals(phase, source_of, landing):
        for d in range(1, blk_count):
            other = blks[blk_count - d]
            blk_copy(phase, d, source_of(other), landing, other, other).wait_recv()

    def req_copy(phase, d, source, landing, slot, other):
        return pltpu.make_async_remote_copy(
            src_ref=source,
            dst_ref=landing.at[slot],
            send_sem=req_send_sem.at[phase, d - 1],
            recv_sem=req_recv_sem.at[phase, d - 1],
            device_id=(other, blk),
            device_id_type=MESH,
        )

    def req_exchange(phase, source_of, landing):
        copies = [
            req_copy(phase, d, source_of(reqs[d]), landing, req, reqs[d])
            for d in range(1, req_count)
        ]
        for copy in copies:
            copy.start()
        return copies

    def req_arrivals(phase, source_of, landing):
        for d in range(1, req_count):
            other = reqs[req_count - d]
            req_copy(phase, d, source_of(other), landing, other, other).wait_recv()

    def all_exchange(phase, source_of, landing):
        for peer in peers:
            pltpu.make_async_remote_copy(
                src_ref=source_of(peer),
                dst_ref=landing.at[me],
                send_sem=all_send_sem.at[phase],
                recv_sem=all_recv_sem.at[phase],
                device_id=peer,
                device_id_type=MESH,
            ).start()

    def finish(copies):
        for copy in copies:
            copy.wait_send()

    row_copies = blk_exchange(0, lambda other: row_send, row_recv)
    for copy in value_loads + late:
        copy.start()
    weight_copies = req_exchange(2, down_block, wdown)
    row_recv[blk] = row_send[...]

    def rotate(part):
        return (part * cosine + pltpu.roll(part, head // 2, 1) * sine).astype(BF16)

    mixed_state = [
        functools.reduce(lambda a, b: a + b, [state[s] * mix_ref[0, s, t] for s in range(count)])
        for t in range(count)
    ]

    row_at = lax.broadcasted_iota(jnp.int32, (heads * group, 1), 0)
    request_at = lax.rem(row_at, group)
    lengths = jnp.zeros((heads * group, 1), jnp.int32)
    for r in range(group):
        lengths = jnp.where(request_at == r, lengths_ref[r], lengths)
    angles = lengths.astype(F32) * freq_ref[...]
    sine, cosine = sine_cosine(angles)
    lane = lax.broadcasted_iota(jnp.int32, (heads * group, head), 1)
    sine = jnp.where(lane < head // 2, -sine, sine)

    line = lax.broadcasted_iota(jnp.int32, (heads * group, lines), 1)
    slot = line // heads
    valid = (slot < lengths) & (line - slot * heads == row_at // group)
    bias[...] = jnp.where(valid, 0.0, -jnp.inf)

    for r in range(group):
        key_loads[r].wait()
        keys_turned[r * head : (r + 1) * head] = jnp.transpose(keys[r])

    blk_arrivals(0, lambda other: row_send, row_recv)
    wide_rows[...] = row_recv[...].astype(F32)
    normed = gather_lanes(wide_rows).astype(BF16)
    projected = []
    for k in range(3):
        loads[k].wait()
        projected.append(jnp.dot(normed, win[k], preferred_element_type=F32))
    finish(row_copies)

    scale = head ** (-0.5)

    def by_head(part):
        return jnp.concatenate([part[:, h * head : (h + 1) * head] for h in range(heads)], axis=0)

    query = rotate(by_head(projected[0]))
    key_new = rotate(by_head(projected[1]))
    value_new = by_head(projected[2]).astype(BF16).astype(F32)
    wide_query = query.astype(F32)
    own = scale * jnp.sum(wide_query * key_new.astype(F32), axis=-1, keepdims=True)
    spread_query = jnp.concatenate(
        [jnp.where(request_at == r, wide_query, 0.0) for r in range(group)], axis=1
    ).astype(BF16)
    scores = jnp.dot(spread_query, keys_turned[...], preferred_element_type=F32)
    scores = scores * scale + bias[...]
    peak = jnp.maximum(jnp.max(scores, axis=-1, keepdims=True), own)
    shares = jnp.exp(scores - peak)
    own_share = jnp.exp(own - peak)
    denom = jnp.sum(shares, axis=-1, keepdims=True) + own_share
    shares = shares.astype(BF16)
    mixed = own_share * value_new
    for r in range(group):
        value_loads[r].wait()
    part = jnp.dot(shares, values[...], preferred_element_type=F32)
    for r in range(group):
        mixed = mixed + jnp.where(
            request_at == r, part[:, r * head : (r + 1) * head], 0.0
        )
    mixed = (mixed / denom).astype(BF16)
    flat = jnp.concatenate(
        [mixed[h * group : (h + 1) * group] for h in range(heads)], axis=1
    )
    late[0].wait()
    scatter_lanes(wide_rows, jnp.dot(flat, wout[...], preferred_element_type=F32))
    attn_send[...] = wide_rows[...].astype(BF16)

    attn_copies = blk_exchange(1, lambda other: attn_send.at[other], attn_recv)
    attn_recv[blk] = attn_send[blk]
    blk_arrivals(1, lambda other: attn_send.at[other], attn_recv)
    attn_out = functools.reduce(lambda a, b: a + b, [attn_recv[j].astype(F32) for j in range(blk_count)])
    state = [mixed_state[t] + depth_ref[0, t] * attn_out for t in range(count)]
    row = functools.reduce(lambda a, b: a + b, [state[s] * width_ref[1, s] for s in range(count)])
    row = normalize(row)
    chunk = norm_send.shape[1]
    for c in range(req_count):
        norm_send[c] = row[c * chunk : (c + 1) * chunk]

    all_exchange(0, lambda peer: norm_send.at[peer[0]], norm_recv)
    norm_recv[me] = norm_send[req]
    finish(attn_copies)
    mixed_state = [
        functools.reduce(lambda a, b: a + b, [state[s] * mix_ref[1, s, t] for s in range(count)])
        for t in range(count)
    ]
    others = pl.ds(0, everyone - 1)
    late[1].wait()
    late[2].wait()
    wait_bytes(norm_recv.at[others], all_recv_sem.at[0])
    columns = gather_lanes(norm_recv).astype(BF16)

    def spread(part, landing):
        for c in range(req_count):
            landing[c] = part[:, c * sub : (c + 1) * sub].astype(BF16)

    def total(landing):
        return functools.reduce(
            lambda a, b: a + b, [landing[c].astype(F32) for c in range(req_count)]
        )

    spread(jnp.dot(columns, wgate[...], preferred_element_type=F32), gate_send)
    gate_copies = req_exchange(0, lambda other: gate_send.at[other], gate_recv)
    spread(jnp.dot(columns, wup[...], preferred_element_type=F32), up_send)
    gate_copies += req_exchange(1, lambda other: up_send.at[other], up_recv)
    gate_recv[req] = gate_send[req]
    up_recv[req] = up_send[req]
    wait_bytes(norm_recv.at[others], all_send_sem.at[0])
    req_arrivals(0, lambda other: gate_send.at[other], gate_recv)
    gate = total(gate_recv)
    gate = gate / (1.0 + jnp.exp(-gate))
    req_arrivals(1, lambda other: up_send.at[other], up_recv)
    hidden = (gate * total(up_recv)).astype(BF16)

    finish(weight_copies)
    late[3].wait()
    req_arrivals(2, down_block, wdown)
    for c in range(req_count):
        part = jnp.dot(hidden, wdown[c], preferred_element_type=F32)
        for k in range(chunk):
            wide_down[:, c * chunk + k, :] = part[:, k * LANES : (k + 1) * LANES]
    down_send[...] = wide_down[...].astype(BF16)
    all_exchange(1, lambda peer: down_send.at[peer[0] * blk_count + peer[1]], down_recv)
    down_recv[me] = down_send[me]
    finish(gate_copies)
    wait_bytes(down_recv.at[others], all_recv_sem.at[1])
    mlp_out = functools.reduce(
        lambda a, b: a + b, [down_recv[j].astype(F32) for j in range(everyone)]
    )
    for t in range(count):
        out_ref[0, t] = mixed_state[t] + depth_ref[1, t] * mlp_out
    wait_bytes(down_recv.at[others], all_send_sem.at[1])


def on_device(
    hyper_state,
    lengths,
    key_cache,
    value_cache,
    attn_in_weight,
    attn_out_weight,
    w_gate,
    w_up,
    w_down,
    width_in,
    stream_mix,
    depth_out,
):
    req_count = lax.axis_size("req")
    blk_count = lax.axis_size("blk")
    everyone = req_count * blk_count
    _, count, width = hyper_state.shape
    group, heads, slots, head = key_cache.shape
    feature_part, hid_part = w_gate.shape
    parts = width // LANES
    sub = hid_part // req_count
    chunk = feature_part // LANES
    freqs = np.exp(np.arange(head // 2) * (-2.0 * math.log(10000.0) / head))
    freqs = np.concatenate([freqs, freqs]).astype(np.float32)[None, :]
    vmem = pl.BlockSpec(memory_space=pltpu.VMEM)
    hbm = pl.BlockSpec(memory_space=pl.ANY)
    like = lambda x: pltpu.VMEM(x.shape, x.dtype)
    scalars = lambda x: pltpu.SMEM(x.shape, x.dtype)
    dma = pltpu.SemaphoreType.DMA
    lines = lambda x: jnp.transpose(x, (0, 2, 1, 3)).reshape(group, slots * heads, head)
    big = [lines(key_cache), lines(value_cache), attn_in_weight, attn_out_weight, w_gate, w_up, w_down]
    return pl.pallas_call(
        functools.partial(layer_kernel, req_count, blk_count),
        out_shape=jax.ShapeDtypeStruct((1, count, parts, LANES), F32),
        in_specs=[hbm] * (6 + len(big)),
        out_specs=vmem,
        scratch_shapes=[
            like(hyper_state),
            scalars(lengths),
            pltpu.VMEM(freqs.shape, F32),
            scalars(width_in),
            scalars(stream_mix),
            scalars(depth_out),
            pltpu.VMEM((heads * group, slots * heads), F32),
            pltpu.VMEM((group * head, slots * heads), BF16),
        ]
        + [like(big[0]), pltpu.VMEM((slots * heads, group * head), BF16)]
        + [like(x) for x in big[2:-1]]
        + [pltpu.VMEM((req_count, sub, w_down.shape[1]), BF16)]
        + [
            pltpu.VMEM((count, parts, LANES), F32),
            pltpu.VMEM((blk_count, parts, LANES), F32),
            pltpu.VMEM((parts, LANES), BF16),
            pltpu.VMEM((blk_count, parts, LANES), BF16),
            pltpu.VMEM((blk_count, parts, LANES), BF16),
            pltpu.VMEM((blk_count, parts, LANES), BF16),
            pltpu.VMEM((req_count, chunk, LANES), F32),
            pltpu.VMEM((everyone, chunk, LANES), F32),
            pltpu.VMEM((req_count, everyone, sub), BF16),
            pltpu.VMEM((req_count, everyone, sub), BF16),
            pltpu.VMEM((req_count, everyone, sub), BF16),
            pltpu.VMEM((req_count, everyone, sub), BF16),
            pltpu.VMEM((everyone, parts, LANES), F32),
            pltpu.VMEM((everyone, parts, LANES), BF16),
            pltpu.VMEM((everyone, parts, LANES), BF16),
            dma((6,)),
            dma((7,)),
            dma((group,)),
            dma((group,)),
            dma((2, blk_count - 1)),
            dma((2, blk_count - 1)),
            dma((3, req_count - 1)),
            dma((3, req_count - 1)),
            dma((2,)),
            dma((2,)),
        ],
        compiler_params=pltpu.CompilerParams(
            collective_id=0, has_side_effects=True, vmem_limit_bytes=56 * 2**20
        ),
        name="layer_step",
    )(hyper_state, lengths, jnp.asarray(freqs), width_in, stream_mix, depth_out, *big).reshape(hyper_state.shape)


def solution(mesh):
    placed = (
        P(("req", "blk"), None, None),
        P("req"),
        P("req", "blk", None, None),
        P("req", "blk", None, None),
        P(None, None, "blk"),
        P("blk", None),
        P("req", "blk"),
        P("req", "blk"),
        P("blk", "req"),
        P(),
        P(),
        P(),
    )
    return jax.shard_map(
        on_device,
        mesh=mesh,
        in_specs=placed,
        out_specs=P(("req", "blk"), None, None),
        check_vma=False,
    )
```
